512 devices in a mesh: src: 32 (over z, x), tgt: 16 (over y, core).
Axes of the slice: x: 4, y: 8, z: 8, core: 2. Of those that a mesh axis runs over, the one named last changes fastest.
Arguments:
- src_emb: float32 [20480, 512], P(('src', 'tgt')), may hold values from -16 to 16
- tgt_emb: float32 [20480, 512], P(('src', 'tgt')), may hold values from -16 to 16
Outputs:
- src_potential: float32 [20480], P(('src', 'tgt'))
- tgt_potential: float32 [20480], P(('src', 'tgt'))
- src_grad: float32 [20480, 512], P(('src', 'tgt'))
- tgt_grad: float32 [20480, 512], P(('src', 'tgt'))
The draws below stay inside these ranges and needn't reach their ends.
All inputs are finite; a program needn't handle non-finite values.
Results may differ from the reference program's by a relative error of at most 0.0003.
Values sent between devices are 32-bit elements; how exact they have to be, the bound alone decides.
No kernel may reach another device: no remote copies, remote signals or barrier semaphores. Data moves between devices by JAX's collectives and lax.ppermute only.
A program may use at most 64 MiB of HBM per device.

```python
import math
import jax
import jax.numpy as jnp
from jax import lax

D = 512
ITERS = 3
NS = 20480
NT = 20480
N_SRC = 32


def embed_draw(key):
    normal_part = jax.random.normal(key, (NS, D), jnp.float32)
    return jnp.clip(normal_part, -6.0, 6.0)


def draw_src_emb(key, part):
    key = jax.random.fold_in(key, 1)
    return embed_draw(key)


def draw_tgt_emb(key, part):
    key = jax.random.fold_in(key, 2)
    return embed_draw(key)


def setup_inputs(seed: int = 0) -> dict:
    arg_keys = jax.random.split(jax.random.key(seed), 3)
    return {
        "src_emb": draw_src_emb(jax.random.fold_in(arg_keys[2], 71), 0),
        "tgt_emb": draw_tgt_emb(jax.random.fold_in(arg_keys[2], 71), 0),
    }


entropy_reg = 0.05


def pair_cost(left, right):
    left_sq = jnp.sum(left * left, axis=1)
    right_sq = jnp.sum(right * right, axis=1)
    cross = jnp.dot(left, right.T, preferred_element_type=jnp.float32, precision=lax.Precision.HIGHEST)
    return (left_sq[:, None] + right_sq[None, :] - 2.0 * cross) / D


def reference(src_emb, tgt_emb):
    block_rows = NS // N_SRC
    src_blocks = src_emb.reshape(N_SRC, block_rows, D)
    tgt_potential = jnp.zeros((NT,), jnp.float32)
    src_potential = jnp.zeros((NS,), jnp.float32)
    for iteration in range(ITERS):
        def row_pass(block):
            scores = (tgt_potential[None, :] - pair_cost(block, tgt_emb)) / entropy_reg
            peak_val = jnp.max(scores, axis=1)
            row_sum = jnp.sum(jnp.exp(scores - peak_val[:, None]), axis=1)
            return -entropy_reg * (peak_val + jnp.log(row_sum) - math.log(NT))

        src_potential = lax.map(row_pass, src_blocks).reshape(NS)
        pot_blocks = src_potential.reshape(N_SRC, block_rows)

        def column_pass(carry, items):
            peak_val, col_sum = carry
            block, pot_block = items
            scores = (pot_block[:, None] - pair_cost(block, tgt_emb)) / entropy_reg
            new_peak = jnp.maximum(peak_val, jnp.max(scores, axis=0))
            col_sum = col_sum * jnp.exp(peak_val - new_peak) + jnp.sum(jnp.exp(scores - new_peak[None, :]), axis=0)
            return (new_peak, col_sum), None

        start_carry = (jnp.full((NT,), -jnp.inf, jnp.float32), jnp.zeros((NT,), jnp.float32))
        (peak_val, col_sum), unused = lax.scan(column_pass, start_carry, (src_blocks, pot_blocks))
        tgt_potential = -entropy_reg * (peak_val + jnp.log(col_sum) - math.log(NS))
    pot_blocks = src_potential.reshape(N_SRC, block_rows)

    def grad_pass(carry, items):
        col_mass, pulled = carry
        block, pot_block = items
        weight = jnp.exp((pot_block[:, None] + tgt_potential[None, :] - pair_cost(block, tgt_emb)) / entropy_reg)
        row_mass = jnp.sum(weight, axis=1)
        pushed = jnp.dot(weight, tgt_emb, preferred_element_type=jnp.float32, precision=lax.Precision.HIGHEST)
        grad_block = (row_mass[:, None] * block - pushed) / NT
        col_mass = col_mass + jnp.sum(weight, axis=0)
        pulled = pulled + jnp.dot(weight.T, block, preferred_element_type=jnp.float32, precision=lax.Precision.HIGHEST)
        return (col_mass, pulled), grad_block

    start_carry = (jnp.zeros((NT,), jnp.float32), jnp.zeros((NT, D), jnp.float32))
    (col_mass, pulled), grad_blocks = lax.scan(grad_pass, start_carry, (src_blocks, pot_blocks))
    src_grad = grad_blocks.reshape(NS, D)
    tgt_grad = (col_mass[:, None] * tgt_emb - pulled) / NS
    return src_potential, tgt_potential, src_grad, tgt_grad
```

```python
import math

import jax
import jax.numpy as jnp
from jax import lax
from jax.experimental import pallas as pl
from jax.experimental.pallas import tpu as pltpu
from jax.sharding import Mesh
from jax.sharding import PartitionSpec as P

ITERS = 3
ENTROPY_REG = 0.05
NZ, NX, NY, NC = 8, 4, 8, 2
LANES = 128

A_OF_X = (0, 0, 1, 1)
B_OF_X = (0, 1, 1, 0)
FLIP_A = [(x, NX - 1 - x) for x in range(NX)]
FLIP_B = [(x, x ^ 1) for x in range(NX)]
SWAP = [(0, 1), (1, 0)]
X_OF_AB = {(A_OF_X[x], B_OF_X[x]): x for x in range(NX)}

ROW_GROUPS = [[X_OF_AB[a, b] * NY + y for a in range(2) for y in range(NY)] for b in range(2)]
COL_GROUPS = [
    [(z * NX + X_OF_AB[a, b]) * NC + c for z in range(NZ) for b in range(2) for c in range(NC)]
    for a in range(2)
]

PAIRS = 4
NEIGHBOUR = [(i, i ^ 1) for i in range(8)]
FIRST = (0, 3)
SECOND = (1, 2)


def ring(step):
    return [(i, (i + step) % 8) for i in range(8)]


def take(buffer, *index):
    start = tuple(index) + (0,) * (buffer.ndim - len(index))
    size = (1,) * len(index) + buffer.shape[len(index):]
    return lax.dynamic_slice(buffer, start, size).reshape(buffer.shape[len(index):])


def gather_ring(shard, axis, at, flip):
    other = lax.ppermute(shard, axis, NEIGHBOUR)
    even = at % 2 == 0
    pair = jnp.concatenate([jnp.where(even, shard, other), jnp.where(even, other, shard)])
    behind = lax.ppermute(pair, axis, ring(2))
    ahead = lax.ppermute(pair, axis, ring(-2))
    across = lax.ppermute(pair, axis, ring(4))
    first = jnp.stack([pair, behind])
    second = jnp.stack([ahead, across])
    return first, lax.ppermute(first, "x", flip), second, lax.ppermute(second, "x", flip)


def tile_kernel(*refs):
    row_refs, col_refs, far_ref = refs[:4], refs[4:8], refs[8]
    src_ref, tgt_ref, cost_ref = refs[9:]
    z, x, y, c = (lax.axis_index(name) for name in ("z", "x", "y", "c"))
    a = x // 2
    b = (x // 2) ^ (x % 2)
    size = row_refs[0].shape[1]
    for half, (mine, other) in enumerate((row_refs[:2], row_refs[2:])):
        for i, step in enumerate((FIRST, SECOND)[half]):
            pair = (y // 2 + step) % PAIRS
            for place, ref in ((a, mine), (1 - a, other)):
                at = pl.multiple_of((place * PAIRS + pair) * size, 8)
                src_ref[pl.ds(at, size), :] = ref[i]
    for half, (mine, other) in enumerate((col_refs[:2], col_refs[2:])):
        for i, step in enumerate((FIRST, SECOND)[half]):
            pair = (z // 2 + step) % PAIRS
            for k, (place, ref) in enumerate(((b, mine), (1 - b, other))):
                at = pl.multiple_of(((c * 2 + place) * PAIRS + pair) * size, 8)
                tgt_ref[pl.ds(at, size), :] = ref[i]
                at = pl.multiple_of((((1 - c) * 2 + place) * PAIRS + pair) * size, 8)
                tgt_ref[pl.ds(at, size), :] = far_ref[half * 4 + k * 2 + i]
    rows, width = src_ref.shape
    cols = tgt_ref.shape[0]
    step = 256
    left = src_ref[...]
    left_sq = jnp.sum(left * left, axis=1, keepdims=True)
    ones = jnp.ones((8, width), jnp.float32)

    @pl.loop(0, cols // step)
    def _(j):
        at = pl.multiple_of(j * step, step)
        right = tgt_ref[pl.ds(at, step), :]
        dims = (((1,), (1,)), ((), ()))
        cross = lax.dot_general(
            src_ref[...],
            right,
            dims,
            precision=lax.Precision.HIGHEST,
            preferred_element_type=jnp.float32,
        )
        right_sq = lax.dot_general(
            ones,
            right * right,
            dims,
            precision=lax.Precision.HIGHEST,
            preferred_element_type=jnp.float32,
        )[:1]
        cost_ref[:, pl.ds(at, step)] = (left_sq + right_sq - 2.0 * cross) / width


def tile(row_pieces, col_pieces, far_piece):
    size, width = row_pieces[0].shape[1:]
    rows, cols = 2 * PAIRS * size, 4 * PAIRS * size
    whole = pl.BlockSpec(memory_space=pltpu.VMEM)
    return pl.pallas_call(
        tile_kernel,
        out_shape=(
            jax.ShapeDtypeStruct((rows, width), jnp.float32),
            jax.ShapeDtypeStruct((cols, width), jnp.float32),
            jax.ShapeDtypeStruct((rows, cols), jnp.float32),
        ),
        in_specs=[whole] * 9,
        out_specs=(whole,) * 3,
        compiler_params=pltpu.CompilerParams(vmem_limit_bytes=48 * 1024 * 1024),
    )(*row_pieces, *col_pieces, far_piece)


def scatter_ring(partial, axis, at, flip, own):
    moves = {2: ring(4), 1: ring(2), 3: ring(-2)}
    here = at // 2
    total = None
    for group in ((2, 1), (3, 0)):
        sent = jnp.stack([take(partial, 1 - own, (here + k) % PAIRS) for k in group])
        got = lax.ppermute(sent, "x", flip)
        for i, k in enumerate(group):
            part = take(partial, own, (here + k) % PAIRS) + got[i]
            if k:
                part = lax.ppermute(part, axis, moves[k])
            total = part if total is None else total + part
    total = total.reshape(2, -1, total.shape[-1])
    return take(total, at % 2) + lax.ppermute(take(total, 1 - at % 2), axis, NEIGHBOUR)


def exchange(local, axes, groups, count):
    size = local.shape[0]
    flat = local.reshape(1, size // LANES, LANES)
    sent = jnp.broadcast_to(flat, (count, size // LANES, LANES))
    got = lax.all_to_all(
        sent, axes, split_axis=0, concat_axis=0, axis_index_groups=groups, tiled=True
    )
    peak = jnp.max(got, axis=0)
    total = jnp.sum(jnp.exp(got - peak[None]), axis=0)
    return (peak + jnp.log(total)).reshape(size)


def local_lse(scores, axis):
    peak = jnp.max(scores, axis=axis, keepdims=True)
    total = jnp.sum(jnp.exp(scores - peak), axis=axis)
    return jnp.squeeze(peak, axis) + jnp.log(total)


def per_device(src_emb, tgt_emb):
    rows, width = src_emb.shape
    z, x, y, c = (lax.axis_index(name) for name in ("z", "x", "y", "c"))
    a = x // 2
    b = (x // 2) ^ (x % 2)
    total_points = rows * NZ * NX * NY * NC
    near, near_flip, rest, rest_flip = gather_ring(tgt_emb, "z", z, FLIP_B)
    col_pieces = (near, near_flip, rest, rest_flip)
    far_piece = lax.ppermute(
        jnp.concatenate([near, near_flip, rest, rest_flip]), "c", SWAP
    )
    near, near_flip, rest, rest_flip = gather_ring(src_emb, "y", y, FLIP_A)
    row_pieces = (near, near_flip, rest, rest_flip)
    src_block, tgt_block, cost = tile(row_pieces, col_pieces, far_piece)
    tgt_pot = jnp.zeros((tgt_block.shape[0],), jnp.float32)
    log_total = math.log(total_points)
    for _ in range(ITERS):
        lse = local_lse((tgt_pot[None, :] - cost) / ENTROPY_REG, 1)
        lse = exchange(lse, ("x", "y"), ROW_GROUPS, 2 * NY)
        src_pot = -ENTROPY_REG * (lse - log_total)
        lse = local_lse((src_pot[:, None] - cost) / ENTROPY_REG, 0)
        lse = exchange(lse, ("z", "x", "c"), COL_GROUPS, 2 * NZ * NC)
        tgt_pot = -ENTROPY_REG * (lse - log_total)
    weight = jnp.exp((src_pot[:, None] + tgt_pot[None, :] - cost) / ENTROPY_REG)
    row_mass = jnp.sum(weight, axis=1)
    col_mass = jnp.sum(weight, axis=0)
    pulled = lax.dot_general(
        weight,
        src_block,
        (((0,), (0,)), ((), ())),
        precision=lax.Precision.HIGH,
        preferred_element_type=jnp.float32,
    )
    tgt_part = (col_mass[:, None] * tgt_block - pulled).reshape(NC, -1, width)
    across = lax.ppermute(take(tgt_part, 1 - c), "c", SWAP)
    tgt_half = (take(tgt_part, c) + across).reshape(2, PAIRS, 2 * rows, width)
    tgt_sum = scatter_ring(tgt_half, "z", z, FLIP_B, b)
    pushed = jnp.dot(
        weight, tgt_block, preferred_element_type=jnp.float32, precision=lax.Precision.HIGH
    )
    src_part = (row_mass[:, None] * src_block - pushed).reshape(2, PAIRS, 2 * rows, width)
    src_sum = scatter_ring(src_part, "y", y, FLIP_A, a)
    src_piece = take(src_pot.reshape(2, NY, rows), a, y)
    tgt_piece = take(tgt_pot.reshape(NC, 2, NZ, rows), c, b, z)
    return src_piece, tgt_piece, src_sum / total_points, tgt_sum / total_points


def solution(mesh):
    grid = Mesh(mesh.devices.reshape(NZ, NX, NY, NC), ("z", "x", "y", "c"))
    split = ("z", "x", "y", "c")
    return jax.shard_map(
        per_device,
        mesh=grid,
        in_specs=(P(split, None), P(split, None)),
        out_specs=(P(split), P(split), P(split, None), P(split, None)),
        check_vma=False,
    )
```

```python
import math

import jax
import jax.numpy as jnp
from jax import lax
from jax.sharding import Mesh
from jax.sharding import PartitionSpec as P

ITERS = 3
ENTROPY_REG = 0.05
NZ, NX, NY, NC = 8, 4, 8, 2
LANES = 128

A_OF_X = (0, 0, 1, 1)
B_OF_X = (0, 1, 1, 0)
FLIP_A = [(x, NX - 1 - x) for x in range(NX)]
FLIP_B = [(x, x ^ 1) for x in range(NX)]
SWAP = [(0, 1), (1, 0)]
X_OF_AB = {(A_OF_X[x], B_OF_X[x]): x for x in range(NX)}

ROW_GROUPS = [[X_OF_AB[a, b] * NY + y for a in range(2) for y in range(NY)] for b in range(2)]
COL_GROUPS = [
    [(z * NX + X_OF_AB[a, b]) * NC + c for z in range(NZ) for b in range(2) for c in range(NC)]
    for a in range(2)
]

SIDE_GROUPS = [
    [z * NX + X_OF_AB[a, b] for z in range(NZ) for b in range(2)] for a in range(2)
]


def take(buffer, index):
    return lax.dynamic_index_in_dim(buffer, index, 0, keepdims=False)


def all_to_all(blocks, axes, groups):
    return lax.all_to_all(
        blocks, axes, split_axis=0, concat_axis=0, axis_index_groups=groups, tiled=True
    )


def gather(shard, axes, groups):
    blocks = jnp.broadcast_to(shard[None], (len(groups[0]),) + shard.shape)
    return all_to_all(blocks, axes, groups).reshape(-1, shard.shape[1])


def scatter(partial, axes, groups):
    count = len(groups[0])
    blocks = partial.reshape(count, partial.shape[0] // count, partial.shape[1])
    return jnp.sum(all_to_all(blocks, axes, groups), axis=0)


def exchange(local, axes, groups, count):
    size = local.shape[0]
    flat = local.reshape(1, size // LANES, LANES)
    sent = jnp.broadcast_to(flat, (count, size // LANES, LANES))
    got = all_to_all(sent, axes, groups)
    peak = jnp.max(got, axis=0)
    total = jnp.sum(jnp.exp(got - peak[None]), axis=0)
    return (peak + jnp.log(total)).reshape(size)


def local_lse(scores, axis):
    peak = jnp.max(scores, axis=axis, keepdims=True)
    total = jnp.sum(jnp.exp(scores - peak), axis=axis)
    return jnp.squeeze(peak, axis) + jnp.log(total)


def per_device(src_emb, tgt_emb):
    rows, width = src_emb.shape
    z, x, y, c = (lax.axis_index(name) for name in ("z", "x", "y", "c"))
    a = x // 2
    b = (x // 2) ^ (x % 2)
    total_points = rows * NZ * NX * NY * NC
    mine = gather(tgt_emb, ("z", "x"), SIDE_GROUPS)
    src_block = gather(src_emb, ("x", "y"), ROW_GROUPS)
    other = lax.ppermute(mine, "c", SWAP)
    tgt_block = jnp.where(
        c == 0, jnp.concatenate([mine, other]), jnp.concatenate([other, mine])
    )
    left_sq = jnp.sum(src_block * src_block, axis=1)
    right_sq = jnp.sum(tgt_block * tgt_block, axis=1)
    cross = jnp.dot(
        src_block,
        tgt_block.T,
        preferred_element_type=jnp.float32,
        precision=lax.Precision.HIGHEST,
    )
    cost = (left_sq[:, None] + right_sq[None, :] - 2.0 * cross) / width
    tgt_pot = jnp.zeros((tgt_block.shape[0],), jnp.float32)
    log_total = math.log(total_points)
    for _ in range(ITERS):
        lse = local_lse((tgt_pot[None, :] - cost) / ENTROPY_REG, 1)
        lse = exchange(lse, ("x", "y"), ROW_GROUPS, 2 * NY)
        src_pot = -ENTROPY_REG * (lse - log_total)
        lse = local_lse((src_pot[:, None] - cost) / ENTROPY_REG, 0)
        lse = exchange(lse, ("z", "x", "c"), COL_GROUPS, 2 * NZ * NC)
        tgt_pot = -ENTROPY_REG * (lse - log_total)
    weight = jnp.exp((src_pot[:, None] + tgt_pot[None, :] - cost) / ENTROPY_REG)
    row_mass = jnp.sum(weight, axis=1)
    col_mass = jnp.sum(weight, axis=0)
    pulled = lax.dot_general(
        weight,
        src_block,
        (((0,), (0,)), ((), ())),
        precision=lax.Precision.HIGH,
        preferred_element_type=jnp.float32,
    )
    tgt_part = (col_mass[:, None] * tgt_block - pulled).reshape(NC, -1, width)
    across = lax.ppermute(take(tgt_part, 1 - c), "c", SWAP)
    tgt_sum = scatter(take(tgt_part, c) + across, ("z", "x"), SIDE_GROUPS)
    pushed = jnp.dot(
        weight, tgt_block, preferred_element_type=jnp.float32, precision=lax.Precision.HIGH
    )
    src_sum = scatter(row_mass[:, None] * src_block - pushed, ("x", "y"), ROW_GROUPS)
    src_piece = take(src_pot.reshape(-1, rows), a * NY + y)
    tgt_piece = take(tgt_pot.reshape(-1, rows), (c * NZ + z) * 2 + b)
    return src_piece, tgt_piece, src_sum / total_points, tgt_sum / total_points


def solution(mesh):
    grid = Mesh(mesh.devices.reshape(NZ, NX, NY, NC), ("z", "x", "y", "c"))
    split = ("z", "x", "y", "c")
    return jax.shard_map(
        per_device,
        mesh=grid,
        in_specs=(P(split, None), P(split, None)),
        out_specs=(P(split), P(split), P(split, None), P(split, None)),
        check_vma=False,
    )
```

```python
import math

import jax
import jax.numpy as jnp
from jax import lax
from jax.experimental import pallas as pl
from jax.experimental.pallas import tpu as pltpu
from jax.sharding import Mesh
from jax.sharding import PartitionSpec as P

ITERS = 3
ENTROPY_REG = 0.05
NZ, NX, NY, NC = 8, 4, 8, 2
LANES = 128

A_OF_X = (0, 0, 1, 1)
B_OF_X = (0, 1, 1, 0)
FLIP_A = [(x, NX - 1 - x) for x in range(NX)]
FLIP_B = [(x, x ^ 1) for x in range(NX)]
SWAP = [(0, 1), (1, 0)]
X_OF_AB = {(A_OF_X[x], B_OF_X[x]): x for x in range(NX)}

ROW_GROUPS = [[X_OF_AB[a, b] * NY + y for a in range(2) for y in range(NY)] for b in range(2)]
COL_GROUPS = [
    [(z * NX + X_OF_AB[a, b]) * NC + c for z in range(NZ) for b in range(2) for c in range(NC)]
    for a in range(2)
]

SIDE_GROUPS = [
    [z * NX + X_OF_AB[a, b] for z in range(NZ) for b in range(2)] for a in range(2)
]


def take(buffer, index):
    return lax.dynamic_index_in_dim(buffer, index, 0, keepdims=False)


def all_to_all(blocks, axes, groups):
    return lax.all_to_all(
        blocks, axes, split_axis=0, concat_axis=0, axis_index_groups=groups, tiled=True
    )


PAIRS = 4
NEIGHBOUR = [(i, i ^ 1) for i in range(8)]
FIRST = (0, 3)
SECOND = (1, 2)
PASSES = ((0, 0), (0, 1), (1, 0), (1, 1), (0, 2), (2, 0))
WHOLE = pl.BlockSpec(memory_space=pltpu.VMEM)
VMEM_LIMIT = 16 * 1024 * 1024


def ring(step):
    return [(i, (i + step) % 8) for i in range(8)]


def gather_blocks(shard, axes, groups):
    blocks = jnp.broadcast_to(shard[None], (len(groups[0]),) + shard.shape)
    return all_to_all(blocks, axes, groups).reshape(-1, shard.shape[1])


def scatter_blocks(partial, axes, groups):
    count = len(groups[0])
    blocks = partial.reshape(count, partial.shape[0] // count, partial.shape[1])
    return jnp.sum(all_to_all(blocks, axes, groups), axis=0)


def gather_ring(shard, axis, at, flip):
    other = lax.ppermute(shard, axis, NEIGHBOUR)
    even = at % 2 == 0
    pair = jnp.concatenate([jnp.where(even, shard, other), jnp.where(even, other, shard)])
    behind = lax.ppermute(pair, axis, ring(2))
    ahead = lax.ppermute(pair, axis, ring(-2))
    across = lax.ppermute(pair, axis, ring(4))
    first = jnp.stack([pair, behind])
    second = jnp.stack([ahead, across])
    return first, lax.ppermute(first, "x", flip), second, lax.ppermute(second, "x", flip)


def scatter_ring(partial, axis, at, flip, own):
    moves = {2: ring(4), 1: ring(2), 3: ring(-2)}
    here = at // 2

    def piece(side, k):
        return take(take(partial, side), (here + k) % PAIRS)

    total = None
    for group in ((2, 1), (3, 0)):
        sent = jnp.stack([piece(1 - own, k) for k in group])
        got = lax.ppermute(sent, "x", flip)
        for i, k in enumerate(group):
            part = piece(own, k) + got[i]
            if k:
                part = lax.ppermute(part, axis, moves[k])
            total = part if total is None else total + part
    total = total.reshape(2, -1, total.shape[-1])
    return take(total, at % 2) + lax.ppermute(take(total, 1 - at % 2), axis, NEIGHBOUR)


def parts_of(values):
    high = values.astype(jnp.bfloat16)
    rest = values - high.astype(jnp.float32)
    mid = rest.astype(jnp.bfloat16)
    low = (rest - mid.astype(jnp.float32)).astype(jnp.bfloat16)
    return high, mid, low


def tile_kernel(*refs):
    row_refs, mine_ref, other_ref = refs[:4], refs[4], refs[5]
    src_ref, tgt_ref, cost_ref, high_ref, mid_ref, low_ref = refs[6:]
    x, y, c = (lax.axis_index(name) for name in ("x", "y", "c"))
    a = x // 2
    size = row_refs[0].shape[1]
    for half, (mine, other) in enumerate((row_refs[:2], row_refs[2:])):
        for i, step in enumerate((FIRST, SECOND)[half]):
            pair = (y // 2 + step) % PAIRS
            for place, ref in ((a, mine), (1 - a, other)):
                at = pl.multiple_of((place * PAIRS + pair) * size, 8)
                src_ref[pl.ds(at, size), :] = ref[i]
    half = mine_ref.shape[0]
    tgt_ref[pl.ds(pl.multiple_of(c * half, 8), half), :] = mine_ref[...]
    tgt_ref[pl.ds(pl.multiple_of((1 - c) * half, 8), half), :] = other_ref[...]
    cols, width = tgt_ref.shape
    step = 256
    left = src_ref[...]
    left_sq = jnp.sum(left * left, axis=1, keepdims=True)
    high_ref[...], mid_ref[...], low_ref[...] = parts_of(left)
    left_parts = (high_ref, mid_ref, low_ref)
    ones = jnp.ones((8, width), jnp.bfloat16)
    dims = (((1,), (1,)), ((), ()))

    def product(p, q):
        return lax.dot_general(p, q, dims, preferred_element_type=jnp.float32)

    @pl.loop(0, cols // step)
    def _(j):
        at = pl.multiple_of(j * step, step)
        right = tgt_ref[pl.ds(at, step), :]
        right_parts = parts_of(right)
        cross = sum(product(left_parts[p][...], right_parts[q]) for p, q in PASSES)
        right_sq = sum(product(ones, part) for part in parts_of(right * right))[:1]
        cost_ref[:, pl.ds(at, step)] = (left_sq + right_sq - 2.0 * cross) / width


def tile(row_pieces, mine, other):
    size, width = row_pieces[0].shape[1:]
    rows, cols = 2 * PAIRS * size, 2 * mine.shape[0]
    part = pltpu.VMEM((rows, width), jnp.bfloat16)
    return pl.pallas_call(
        tile_kernel,
        out_shape=(
            jax.ShapeDtypeStruct((rows, width), jnp.float32),
            jax.ShapeDtypeStruct((cols, width), jnp.float32),
            jax.ShapeDtypeStruct((rows, cols), jnp.float32),
        ),
        in_specs=[WHOLE] * 6,
        out_specs=(WHOLE,) * 3,
        scratch_shapes=[part] * 3,
        compiler_params=pltpu.CompilerParams(vmem_limit_bytes=VMEM_LIMIT),
    )(*row_pieces, mine, other)


def exchange(local, axes, groups, count):
    size = local.shape[0]
    flat = local.reshape(1, size // LANES, LANES)
    sent = jnp.broadcast_to(flat, (count, size // LANES, LANES))
    got = all_to_all(sent, axes, groups)
    peak = jnp.max(got, axis=0)
    total = jnp.sum(jnp.exp(got - peak[None]), axis=0)
    return (peak + jnp.log(total)).reshape(size)


def local_lse(scores, axis):
    peak = jnp.max(scores, axis=axis, keepdims=True)
    total = jnp.sum(jnp.exp(scores - peak), axis=axis)
    return jnp.squeeze(peak, axis) + jnp.log(total)


def per_device(src_emb, tgt_emb):
    rows, width = src_emb.shape
    z, x, y, c = (lax.axis_index(name) for name in ("z", "x", "y", "c"))
    a = x // 2
    b = (x // 2) ^ (x % 2)
    total_points = rows * NZ * NX * NY * NC
    mine = gather_blocks(tgt_emb, ("z", "x"), SIDE_GROUPS)
    row_pieces = gather_ring(src_emb, "y", y, FLIP_A)
    mine, row_pieces = lax.optimization_barrier((mine, row_pieces))
    other = lax.ppermute(mine, "c", SWAP)
    src_block, tgt_block, cost = tile(row_pieces, mine, other)
    tgt_pot = jnp.zeros((tgt_block.shape[0],), jnp.float32)
    log_total = math.log(total_points)
    for _ in range(ITERS):
        lse = local_lse((tgt_pot[None, :] - cost) / ENTROPY_REG, 1)
        lse = exchange(lse, ("x", "y"), ROW_GROUPS, 2 * NY)
        src_pot = -ENTROPY_REG * (lse - log_total)
        lse = local_lse((src_pot[:, None] - cost) / ENTROPY_REG, 0)
        lse = exchange(lse, ("z", "x", "c"), COL_GROUPS, 2 * NZ * NC)
        tgt_pot = -ENTROPY_REG * (lse - log_total)
    weight = jnp.exp((src_pot[:, None] + tgt_pot[None, :] - cost) / ENTROPY_REG)
    row_mass = jnp.sum(weight, axis=1)
    col_mass = jnp.sum(weight, axis=0)
    pulled = lax.dot_general(
        weight,
        src_block,
        (((0,), (0,)), ((), ())),
        precision=lax.Precision.HIGH,
        preferred_element_type=jnp.float32,
    )
    tgt_part = (col_mass[:, None] * tgt_block - pulled).reshape(NC, -1, width)
    across = lax.ppermute(take(tgt_part, 1 - c), "c", SWAP)
    tgt_sum = scatter_blocks(take(tgt_part, c) + across, ("z", "x"), SIDE_GROUPS)
    pushed = jnp.dot(
        weight, tgt_block, preferred_element_type=jnp.float32, precision=lax.Precision.HIGH
    )
    src_part = (row_mass[:, None] * src_block - pushed).reshape(2, PAIRS, 2 * rows, width)
    src_sum = scatter_ring(src_part, "y", y, FLIP_A, a)
    src_piece = take(src_pot.reshape(-1, rows), a * NY + y)
    tgt_piece = take(tgt_pot.reshape(-1, rows), (c * NZ + z) * 2 + b)
    return src_piece, tgt_piece, src_sum / total_points, tgt_sum / total_points


def solution(mesh):
    grid = Mesh(mesh.devices.reshape(NZ, NX, NY, NC), ("z", "x", "y", "c"))
    split = ("z", "x", "y", "c")
    return jax.shard_map(
        per_device,
        mesh=grid,
        in_specs=(P(split, None), P(split, None)),
        out_specs=(P(split), P(split), P(split, None), P(split, None)),
        check_vma=False,
    )
```

```python
import math

import jax
import jax.numpy as jnp
from jax import lax
from jax.experimental import pallas as pl
from jax.experimental.pallas import tpu as pltpu
from jax.sharding import Mesh
from jax.sharding import PartitionSpec as P

ITERS = 3
ENTROPY_REG = 0.05
NZ, NX, NY, NC = 8, 4, 8, 2
LANES = 128

A_OF_X = (0, 0, 1, 1)
B_OF_X = (0, 1, 1, 0)
FLIP_A = [(x, NX - 1 - x) for x in range(NX)]
FLIP_B = [(x, x ^ 1) for x in range(NX)]
SWAP = [(0, 1), (1, 0)]
X_OF_AB = {(A_OF_X[x], B_OF_X[x]): x for x in range(NX)}

ROW_GROUPS = [[X_OF_AB[a, b] * NY + y for a in range(2) for y in range(NY)] for b in range(2)]
COL_GROUPS = [
    [(z * NX + X_OF_AB[a, b]) * NC + c for z in range(NZ) for b in range(2) for c in range(NC)]
    for a in range(2)
]

SIDE_GROUPS = [
    [z * NX + X_OF_AB[a, b] for z in range(NZ) for b in range(2)] for a in range(2)
]


def take(buffer, index):
    return lax.dynamic_index_in_dim(buffer, index, 0, keepdims=False)


def all_to_all(blocks, axes, groups):
    return lax.all_to_all(
        blocks, axes, split_axis=0, concat_axis=0, axis_index_groups=groups, tiled=True
    )


STEPS = (4, 3, 5, 2, 6, 1, 7)
PASSES = ((0, 0), (0, 1), (1, 0), (1, 1), (0, 2), (2, 0))
IN_HBM = pl.BlockSpec(memory_space=pltpu.HBM)
WHOLE = pl.BlockSpec(memory_space=pltpu.VMEM)
VMEM_LIMIT = 24 * 1024 * 1024


def ring(step):
    return [(i, (i + step) % 8) for i in range(8)]


def gather_blocks(shard, axes, groups):
    blocks = jnp.broadcast_to(shard[None], (len(groups[0]),) + shard.shape)
    return all_to_all(blocks, axes, groups).reshape(-1, shard.shape[1])


def scatter_blocks(partial, axes, groups):
    count = len(groups[0])
    blocks = partial.reshape(count, partial.shape[0] // count, partial.shape[1])
    return jnp.sum(all_to_all(blocks, axes, groups), axis=0)


def gather_ring(shard, a):
    other = lax.ppermute(shard, "x", FLIP_A)
    pair = jnp.stack([jnp.where(a == 0, shard, other), jnp.where(a == 0, other, shard)])
    return (pair,) + tuple(lax.ppermute(pair, "y", ring(k)) for k in STEPS)


def scatter_ring(partial, y, a):
    total = take(partial, y)
    for k in STEPS:
        total = total + lax.ppermute(take(partial, (y + k) % NY), "y", ring(k))
    return take(total, a) + lax.ppermute(take(total, 1 - a), "x", FLIP_A)


def parts_of(values):
    high = values.astype(jnp.bfloat16)
    rest = values - high.astype(jnp.float32)
    mid = rest.astype(jnp.bfloat16)
    low = (rest - mid.astype(jnp.float32)).astype(jnp.bfloat16)
    return high, mid, low


def product(p, q, contract):
    return lax.dot_general(
        p, q, ((contract[:1], contract[1:]), ((), ())), preferred_element_type=jnp.float32
    )


def three_products(p, q, contract):
    return (
        product(p[0], q[0], contract)
        + product(p[0], q[1], contract)
        + product(p[1], q[0], contract)
    )


def tile_kernel(*refs):
    row_refs, mine_ref, other_ref = refs[:8], refs[8], refs[9]
    src_out, tgt_out, cost_ref, src_ref, tgt_ref = refs[10:15]
    high_ref, mid_ref, low_ref, row_sem, col_sem, out_sem = refs[15:]
    y, c = lax.axis_index("y"), lax.axis_index("c")
    size = row_refs[0].shape[0]
    row_copies = []
    for i, step in enumerate((0,) + STEPS):
        at = pl.multiple_of((y + NY - step) % NY * size, 8)
        row_copies.append(
            pltpu.make_async_copy(row_refs[i], src_ref.at[pl.ds(at, size)], row_sem.at[i])
        )
    half = mine_ref.shape[0]
    col_copies = []
    for i, (place, ref) in enumerate(((c, mine_ref), (1 - c, other_ref))):
        at = pl.multiple_of(place * half, 8)
        col_copies.append(
            pltpu.make_async_copy(ref, tgt_ref.at[pl.ds(at, half)], col_sem.at[i])
        )
    for copy in row_copies + col_copies:
        copy.start()
    for copy in row_copies:
        copy.wait()
    cols, width = tgt_ref.shape
    step = 256
    left = src_ref[...]
    left_sq = jnp.sum(left * left, axis=1, keepdims=True)
    high_ref[...], mid_ref[...], low_ref[...] = parts_of(left)
    left_parts = (high_ref, mid_ref, low_ref)
    ones = jnp.ones((8, width), jnp.bfloat16)
    for copy in col_copies:
        copy.wait()
    out_copies = (
        pltpu.make_async_copy(src_ref, src_out, out_sem.at[0]),
        pltpu.make_async_copy(tgt_ref, tgt_out, out_sem.at[1]),
    )
    for copy in out_copies:
        copy.start()

    @pl.loop(0, cols // step)
    def _(j):
        at = pl.multiple_of(j * step, step)
        right = tgt_ref[pl.ds(at, step), :]
        right_parts = parts_of(right)
        cross = sum(product(left_parts[p][...], right_parts[q], (1, 1)) for p, q in PASSES)
        right_sq = sum(product(ones, part, (1, 1)) for part in parts_of(right * right))[:1]
        cost_ref[:, pl.ds(at, step)] = (left_sq + right_sq - 2.0 * cross) / width

    for copy in out_copies:
        copy.wait()


def tile(row_pieces, mine, other):
    size, width = row_pieces[0].shape
    rows, cols = NY * size, 2 * mine.shape[0]
    part = pltpu.VMEM((rows, width), jnp.bfloat16)
    return pl.pallas_call(
        tile_kernel,
        out_shape=(
            jax.ShapeDtypeStruct((rows, width), jnp.float32),
            jax.ShapeDtypeStruct((cols, width), jnp.float32),
            jax.ShapeDtypeStruct((rows, cols), jnp.float32),
        ),
        in_specs=[IN_HBM] * 10,
        out_specs=(IN_HBM, IN_HBM, WHOLE),
        scratch_shapes=[
            pltpu.VMEM((rows, width), jnp.float32),
            pltpu.VMEM((cols, width), jnp.float32),
            part,
            part,
            part,
            pltpu.SemaphoreType.DMA((NY,)),
            pltpu.SemaphoreType.DMA((2,)),
            pltpu.SemaphoreType.DMA((2,)),
        ],
        compiler_params=pltpu.CompilerParams(vmem_limit_bytes=VMEM_LIMIT),
    )(*row_pieces, mine, other)


def half_of(high_ref, mid_ref, place):
    size = high_ref.shape[1] // 2
    at = pl.ds(pl.multiple_of(place * size, LANES), size)
    return high_ref[:, at], mid_ref[:, at]


def pull(weight_parts, src_ref, tgt):
    src_parts = parts_of(src_ref[...])
    pulled = three_products(weight_parts, src_parts, (0, 0))
    ones = jnp.ones((src_ref.shape[0], LANES), jnp.bfloat16)
    mass = sum(product(part, ones, (0, 0)) for part in weight_parts)[:, :1]
    return mass * tgt - pulled


def send_kernel(
    src_pot_ref, tgt_pot_ref, cost_ref, src_hbm, tgt_hbm, sent_ref, high_ref, mid_ref,
    src_ref, tgt_ref, sem,
):
    rows, cols = cost_ref.shape
    half = cols // 2
    place = 1 - lax.axis_index("c")
    there = tgt_hbm.at[pl.ds(pl.multiple_of(place * half, 8), half)]
    copies = (
        pltpu.make_async_copy(src_hbm, src_ref, sem.at[0]),
        pltpu.make_async_copy(there, tgt_ref, sem.at[1]),
    )
    for copy in copies:
        copy.start()
    lane = lax.broadcasted_iota(jnp.int32, (LANES, LANES), 1)
    sub = lax.broadcasted_iota(jnp.int32, (LANES, LANES), 0)
    for i in range(rows // LANES):
        row = jnp.broadcast_to(src_pot_ref[i : i + 1, :], (LANES, LANES))
        column = jnp.sum(jnp.where(lane == sub, row, 0.0), axis=1, keepdims=True)
        at = slice(i * LANES, (i + 1) * LANES)
        for j in range(cols // LANES):
            to = slice(j * LANES, (j + 1) * LANES)
            total = column + tgt_pot_ref[j : j + 1, :] - cost_ref[at, to]
            weight = jnp.exp(total / ENTROPY_REG)
            high = weight.astype(jnp.bfloat16)
            high_ref[at, to] = high
            mid_ref[at, to] = (weight - high.astype(jnp.float32)).astype(jnp.bfloat16)
    for copy in copies:
        copy.wait()
    sent_ref[...] = pull(half_of(high_ref, mid_ref, place), src_ref, tgt_ref[...])


def push_kernel(high_ref, mid_ref, src_ref, tgt_ref, out_ref):
    weight_parts = high_ref[...], mid_ref[...]
    pushed = three_products(weight_parts, parts_of(tgt_ref[...]), (1, 0))
    ones = jnp.ones((tgt_ref.shape[0], LANES), jnp.bfloat16)
    mass = sum(product(part, ones, (1, 0)) for part in weight_parts)[:, :1]
    out_ref[...] = mass * src_ref[...] - pushed


def keep_kernel(high_ref, mid_ref, src_ref, tgt_ref, came_ref, out_ref):
    place = lax.axis_index("c")
    half = came_ref.shape[0]
    tgt = tgt_ref[pl.ds(pl.multiple_of(place * half, 8), half), :]
    out_ref[...] = pull(half_of(high_ref, mid_ref, place), src_ref, tgt) + came_ref[...]


def on_tile(kernel, out_shape, *args):
    return pl.pallas_call(
        kernel,
        out_shape=out_shape,
        in_specs=[WHOLE] * len(args),
        out_specs=jax.tree.map(lambda _: WHOLE, out_shape),
        compiler_params=pltpu.CompilerParams(vmem_limit_bytes=VMEM_LIMIT),
    )(*args)


def exchange(local, axes, groups, count):
    size = local.shape[0]
    flat = local.reshape(1, size // LANES, LANES)
    sent = jnp.broadcast_to(flat, (count, size // LANES, LANES))
    got = all_to_all(sent, axes, groups)
    peak = jnp.max(got, axis=0)
    total = jnp.sum(jnp.exp(got - peak[None]), axis=0)
    return peak + jnp.log(total)


def local_lse(scores, axis):
    peak = jnp.max(scores, axis=axis, keepdims=True)
    total = jnp.sum(jnp.exp(scores - peak), axis=axis)
    return jnp.squeeze(peak, axis) + jnp.log(total)


def per_device(src_emb, tgt_emb):
    rows, width = src_emb.shape
    z, x, y, c = (lax.axis_index(name) for name in ("z", "x", "y", "c"))
    a = x // 2
    b = (x // 2) ^ (x % 2)
    total_points = rows * NZ * NX * NY * NC
    mine = gather_blocks(tgt_emb, ("z", "x"), SIDE_GROUPS)
    row_pieces = tuple(piece.reshape(-1, width) for piece in gather_ring(src_emb, a))
    mine, row_pieces = lax.optimization_barrier((mine, row_pieces))
    other = lax.ppermute(mine, "c", SWAP)
    src_block, tgt_block, cost = tile(row_pieces, mine, other)
    tile_rows, tile_cols = cost.shape
    tgt_pot = jnp.zeros((tile_cols,), jnp.float32)
    log_total = math.log(total_points)
    for _ in range(ITERS):
        lse = local_lse((tgt_pot.reshape(1, tile_cols) - cost) / ENTROPY_REG, 1)
        lse = exchange(lse, ("x", "y"), ROW_GROUPS, 2 * NY)
        src_pot = -ENTROPY_REG * (lse - log_total)
        lse = local_lse((src_pot.reshape(tile_rows, 1) - cost) / ENTROPY_REG, 0)
        lse = exchange(lse, ("z", "x", "c"), COL_GROUPS, 2 * NZ * NC)
        tgt_pot = -ENTROPY_REG * (lse - log_total)
    part = jax.ShapeDtypeStruct(cost.shape, jnp.bfloat16)
    block = jax.ShapeDtypeStruct(src_block.shape, jnp.float32)
    half = jax.ShapeDtypeStruct(mine.shape, jnp.float32)
    sent, high, mid = pl.pallas_call(
        send_kernel,
        out_shape=(half, part, part),
        in_specs=[WHOLE] * 3 + [IN_HBM] * 2,
        out_specs=(WHOLE,) * 3,
        scratch_shapes=[
            pltpu.VMEM(src_block.shape, jnp.float32),
            pltpu.VMEM(mine.shape, jnp.float32),
            pltpu.SemaphoreType.DMA((2,)),
        ],
        compiler_params=pltpu.CompilerParams(vmem_limit_bytes=VMEM_LIMIT),
    )(src_pot, tgt_pot, cost, src_block, tgt_block)
    came = lax.ppermute(sent, "c", SWAP)
    src_part = on_tile(push_kernel, block, high, mid, src_block, tgt_block)
    came, src_part = lax.optimization_barrier((came, src_part))
    tgt_half = on_tile(keep_kernel, half, high, mid, src_block, tgt_block, came)
    tgt_sum = scatter_blocks(tgt_half, ("z", "x"), SIDE_GROUPS)
    src_sum = scatter_ring(src_part.reshape(NY, 2, rows, width), y, a)
    src_piece = take(src_pot.reshape(-1, rows), y * 2 + a)
    tgt_piece = take(tgt_pot.reshape(-1, rows), (c * NZ + z) * 2 + b)
    return src_piece, tgt_piece, src_sum / total_points, tgt_sum / total_points


def solution(mesh):
    grid = Mesh(mesh.devices.reshape(NZ, NX, NY, NC), ("z", "x", "y", "c"))
    split = ("z", "x", "y", "c")
    return jax.shard_map(
        per_device,
        mesh=grid,
        in_specs=(P(split, None), P(split, None)),
        out_specs=(P(split), P(split), P(split, None), P(split, None)),
        check_vma=False,
    )
```

```python
import math

import jax
import jax.numpy as jnp
from jax import lax
from jax.experimental import pallas as pl
from jax.experimental.pallas import tpu as pltpu
from jax.sharding import Mesh
from jax.sharding import PartitionSpec as P

ITERS = 3
ENTROPY_REG = 0.05
NZ, NX, NY, NC = 8, 4, 8, 2
LANES = 128

A_OF_X = (0, 0, 1, 1)
B_OF_X = (0, 1, 1, 0)
FLIP_A = [(x, NX - 1 - x) for x in range(NX)]
FLIP_B = [(x, x ^ 1) for x in range(NX)]
SWAP = [(0, 1), (1, 0)]
X_OF_AB = {(A_OF_X[x], B_OF_X[x]): x for x in range(NX)}

ROW_GROUPS = [[X_OF_AB[a, b] * NY + y for a in range(2) for y in range(NY)] for b in range(2)]
COL_GROUPS = [
    [(z * NX + X_OF_AB[a, b]) * NC + c for z in range(NZ) for b in range(2) for c in range(NC)]
    for a in range(2)
]

SIDE_GROUPS = [
    [z * NX + X_OF_AB[a, b] for z in range(NZ) for b in range(2)] for a in range(2)
]


def take(buffer, index):
    return lax.dynamic_index_in_dim(buffer, index, 0, keepdims=False)


def all_to_all(blocks, axes, groups):
    return lax.all_to_all(
        blocks, axes, split_axis=0, concat_axis=0, axis_index_groups=groups, tiled=True
    )


NEAR = (0, 1, 7, 2)
FAR = (6, 3, 5, 4)
SEND_FIRST = (4, 3, 5, 2)
SEND_LAST = (6, 1, 7, 0)
PASSES = ((0, 0), (0, 1), (1, 0), (1, 1), (0, 2), (2, 0))
IN_HBM = pl.BlockSpec(memory_space=pltpu.HBM)
WHOLE = pl.BlockSpec(memory_space=pltpu.VMEM)
VMEM_LIMIT = 24 * 1024 * 1024


def ring(step):
    return [(i, (i + step) % 8) for i in range(8)]


def gather_blocks(shard, axes, groups):
    blocks = jnp.broadcast_to(shard[None], (len(groups[0]),) + shard.shape)
    return all_to_all(blocks, axes, groups).reshape(-1, shard.shape[1])


def scatter_blocks(partial, axes, groups):
    count = len(groups[0])
    blocks = partial.reshape(count, partial.shape[0] // count, partial.shape[1])
    return jnp.sum(all_to_all(blocks, axes, groups), axis=0)


def gather_ring(shard):
    behind = {k: lax.ppermute(shard, "y", ring(k)) if k else shard for k in NEAR + FAR}
    pieces = []
    for group in (NEAR, FAR):
        mine = jnp.stack([behind[k] for k in group])
        pieces += [mine, lax.ppermute(mine, "x", FLIP_A)]
    return pieces


def scatter_ring(sent, own):
    total = None
    for group, there, here in zip((SEND_FIRST, SEND_LAST), sent, own):
        here = here + lax.ppermute(there, "x", FLIP_A)
        for i, k in enumerate(group):
            part = lax.ppermute(here[i], "y", ring(k)) if k else here[i]
            total = part if total is None else total + part
    return total


def parts_of(values):
    high = values.astype(jnp.bfloat16)
    rest = values - high.astype(jnp.float32)
    mid = rest.astype(jnp.bfloat16)
    low = (rest - mid.astype(jnp.float32)).astype(jnp.bfloat16)
    return high, mid, low


def product(p, q, contract):
    return lax.dot_general(
        p, q, ((contract[:1], contract[1:]), ((), ())), preferred_element_type=jnp.float32
    )


def three_products(p, q, contract):
    return (
        product(p[0], q[0], contract)
        + product(p[0], q[1], contract)
        + product(p[1], q[0], contract)
    )


def cost_half(left_parts, left_sq, right_ref, cost_ref, place):
    cols, width = right_ref.shape
    right = right_ref[...]
    right_parts = parts_of(right)
    cross = sum(product(left_parts[p][...], right_parts[q], (1, 1)) for p, q in PASSES)
    ones = jnp.ones((8, width), jnp.bfloat16)
    right_sq = sum(product(ones, part, (1, 1)) for part in parts_of(right * right))[:1]
    at = pl.ds(pl.multiple_of(place * cols, LANES), cols)
    cost_ref[:, at] = (left_sq + right_sq - 2.0 * cross) / width


def mine_kernel(*refs):
    pieces, mine_hbm = refs[:4], refs[4]
    src_out, high_ref, mid_ref, low_ref, sq_ref, cost_ref = refs[5:11]
    src_ref, mine_ref, sem, out_sem = refs[11:]
    x, y, c = (lax.axis_index(name) for name in ("x", "y", "c"))
    a = x // 2
    size = pieces[0].shape[1]
    copies = [pltpu.make_async_copy(mine_hbm, mine_ref, sem.at[2 * NY])]
    for half, group in enumerate((NEAR, FAR)):
        for side, place in enumerate((a, 1 - a)):
            for i, k in enumerate(group):
                at = pl.multiple_of(((y + NY - k) % NY * 2 + place) * size, 8)
                copies.append(
                    pltpu.make_async_copy(
                        pieces[half * 2 + side].at[i],
                        src_ref.at[pl.ds(at, size)],
                        sem.at[(half * 2 + side) * 4 + i],
                    )
                )
    for copy in copies:
        copy.start()
    for copy in copies:
        copy.wait()
    out = pltpu.make_async_copy(src_ref, src_out, out_sem)
    out.start()
    left = src_ref[...]
    left_sq = jnp.sum(left * left, axis=1, keepdims=True)
    sq_ref[...] = left_sq
    high_ref[...], mid_ref[...], low_ref[...] = parts_of(left)
    cost_half((high_ref, mid_ref, low_ref), left_sq, mine_ref, cost_ref, c)
    out.wait()


def other_kernel(high_ref, mid_ref, low_ref, sq_ref, other_ref, same_ref, cost_ref):
    del same_ref
    place = 1 - lax.axis_index("c")
    cost_half((high_ref, mid_ref, low_ref), sq_ref[...], other_ref, cost_ref, place)


def tile(row_pieces, mine):
    size, width = row_pieces[0].shape[1:]
    rows, cols = 2 * NY * size, 2 * mine.shape[0]
    part = jax.ShapeDtypeStruct((rows, width), jnp.bfloat16)
    src_block, high, mid, low, left_sq, cost = pl.pallas_call(
        mine_kernel,
        out_shape=(
            jax.ShapeDtypeStruct((rows, width), jnp.float32),
            part,
            part,
            part,
            jax.ShapeDtypeStruct((rows, 1), jnp.float32),
            jax.ShapeDtypeStruct((rows, cols), jnp.float32),
        ),
        in_specs=[IN_HBM] * 5,
        out_specs=(IN_HBM,) + (WHOLE,) * 5,
        scratch_shapes=[
            pltpu.VMEM((rows, width), jnp.float32),
            pltpu.VMEM(mine.shape, jnp.float32),
            pltpu.SemaphoreType.DMA((2 * NY + 1,)),
            pltpu.SemaphoreType.DMA,
        ],
        compiler_params=pltpu.CompilerParams(vmem_limit_bytes=VMEM_LIMIT),
    )(*row_pieces, mine)
    other = lax.ppermute(mine, "c", SWAP)
    cost = pl.pallas_call(
        other_kernel,
        out_shape=jax.ShapeDtypeStruct((rows, cols), jnp.float32),
        in_specs=[WHOLE] * 6,
        out_specs=WHOLE,
        input_output_aliases={5: 0},
        compiler_params=pltpu.CompilerParams(vmem_limit_bytes=VMEM_LIMIT),
    )(high, mid, low, left_sq, other, cost)
    return src_block, other, cost


def half_of(high_ref, mid_ref, place):
    size = high_ref.shape[1] // 2
    at = pl.ds(pl.multiple_of(place * size, LANES), size)
    return high_ref[:, at], mid_ref[:, at]


def pull(weight_parts, src_ref, tgt):
    pulled = three_products(weight_parts, parts_of(src_ref[...]), (0, 0))
    ones = jnp.ones((src_ref.shape[0], LANES), jnp.bfloat16)
    mass = sum(product(part, ones, (0, 0)) for part in weight_parts)[:, :1]
    return mass * tgt - pulled


def send_kernel(
    src_pot_ref, tgt_pot_ref, cost_ref, src_hbm, other_hbm, sent_ref, high_ref, mid_ref,
    src_ref, tgt_ref, sem,
):
    rows, cols = cost_ref.shape
    copies = (
        pltpu.make_async_copy(src_hbm, src_ref, sem.at[0]),
        pltpu.make_async_copy(other_hbm, tgt_ref, sem.at[1]),
    )
    for copy in copies:
        copy.start()
    lane = lax.broadcasted_iota(jnp.int32, (LANES, LANES), 1)
    sub = lax.broadcasted_iota(jnp.int32, (LANES, LANES), 0)
    for i in range(rows // LANES):
        row = jnp.broadcast_to(src_pot_ref[i : i + 1, :], (LANES, LANES))
        column = jnp.sum(jnp.where(lane == sub, row, 0.0), axis=1, keepdims=True)
        at = slice(i * LANES, (i + 1) * LANES)
        for j in range(cols // LANES):
            to = slice(j * LANES, (j + 1) * LANES)
            total = column + tgt_pot_ref[j : j + 1, :] - cost_ref[at, to]
            weight = jnp.exp(total / ENTROPY_REG)
            high = weight.astype(jnp.bfloat16)
            high_ref[at, to] = high
            mid_ref[at, to] = (weight - high.astype(jnp.float32)).astype(jnp.bfloat16)
    for copy in copies:
        copy.wait()
    place = 1 - lax.axis_index("c")
    sent_ref[...] = pull(half_of(high_ref, mid_ref, place), src_ref, tgt_ref[...])


def push_kernel(high_ref, mid_ref, src_ref, mine_ref, other_ref, *out_refs):
    sent_refs, own_refs, part_ref = out_refs[:2], out_refs[2:4], out_refs[4]
    x, y, c = (lax.axis_index(name) for name in ("x", "y", "c"))
    a = x // 2
    ones = jnp.ones((mine_ref.shape[0], LANES), jnp.bfloat16)
    pushed, mass = 0.0, 0.0
    for place, ref in ((c, mine_ref), (1 - c, other_ref)):
        weight_parts = half_of(high_ref, mid_ref, place)
        pushed += three_products(weight_parts, parts_of(ref[...]), (1, 0))
        mass += sum(product(part, ones, (1, 0)) for part in weight_parts)
    part_ref[...] = mass[:, :1] * src_ref[...] - pushed
    size = own_refs[0].shape[1]
    for half, group in enumerate((SEND_FIRST, SEND_LAST)):
        for i, k in enumerate(group):
            for ref, place in ((own_refs[half], a), (sent_refs[half], 1 - a)):
                at = pl.multiple_of(((y + k) % NY * 2 + place) * size, 8)
                ref[i] = part_ref[pl.ds(at, size), :]


def keep_kernel(high_ref, mid_ref, src_ref, mine_ref, came_ref, out_ref):
    place = lax.axis_index("c")
    kept = pull(half_of(high_ref, mid_ref, place), src_ref, mine_ref[...])
    out_ref[...] = kept + came_ref[...]


def on_tile(kernel, out_shape, scratch, *args):
    return pl.pallas_call(
        kernel,
        out_shape=out_shape,
        in_specs=[WHOLE] * len(args),
        out_specs=jax.tree.map(lambda _: WHOLE, out_shape),
        scratch_shapes=scratch,
        compiler_params=pltpu.CompilerParams(vmem_limit_bytes=VMEM_LIMIT),
    )(*args)


def exchange(local, axes, groups, count):
    size = local.shape[0]
    flat = local.reshape(1, size // LANES, LANES)
    sent = jnp.broadcast_to(flat, (count, size // LANES, LANES))
    got = all_to_all(sent, axes, groups)
    peak = jnp.max(got, axis=0)
    total = jnp.sum(jnp.exp(got - peak[None]), axis=0)
    return peak + jnp.log(total)


def local_lse(scores, axis):
    peak = jnp.max(scores, axis=axis, keepdims=True)
    total = jnp.sum(jnp.exp(scores - peak), axis=axis)
    return jnp.squeeze(peak, axis) + jnp.log(total)


def per_device(src_emb, tgt_emb):
    rows, width = src_emb.shape
    z, x, y, c = (lax.axis_index(name) for name in ("z", "x", "y", "c"))
    a = x // 2
    b = (x // 2) ^ (x % 2)
    total_points = rows * NZ * NX * NY * NC
    mine = gather_blocks(tgt_emb, ("z", "x"), SIDE_GROUPS)
    row_pieces = gather_ring(src_emb)
    mine, *row_pieces[1:3] = lax.optimization_barrier((mine, *row_pieces[1:3]))
    src_block, other, cost = tile(row_pieces, mine)
    tile_rows, tile_cols = cost.shape
    tgt_pot = jnp.zeros((tile_cols,), jnp.float32)
    log_total = math.log(total_points)
    for _ in range(ITERS):
        lse = local_lse((tgt_pot.reshape(1, tile_cols) - cost) / ENTROPY_REG, 1)
        lse = exchange(lse, ("x", "y"), ROW_GROUPS, 2 * NY)
        src_pot = -ENTROPY_REG * (lse - log_total)
        lse = local_lse((src_pot.reshape(tile_rows, 1) - cost) / ENTROPY_REG, 0)
        lse = exchange(lse, ("z", "x", "c"), COL_GROUPS, 2 * NZ * NC)
        tgt_pot = -ENTROPY_REG * (lse - log_total)
    part = jax.ShapeDtypeStruct(cost.shape, jnp.bfloat16)
    half = jax.ShapeDtypeStruct(mine.shape, jnp.float32)
    sent, high, mid = pl.pallas_call(
        send_kernel,
        out_shape=(half, part, part),
        in_specs=[WHOLE] * 3 + [IN_HBM] * 2,
        out_specs=(WHOLE,) * 3,
        scratch_shapes=[
            pltpu.VMEM(src_block.shape, jnp.float32),
            pltpu.VMEM(mine.shape, jnp.float32),
            pltpu.SemaphoreType.DMA((2,)),
        ],
        compiler_params=pltpu.CompilerParams(vmem_limit_bytes=VMEM_LIMIT),
    )(src_pot, tgt_pot, cost, src_block, other)
    came = lax.ppermute(sent, "c", SWAP)
    four = jax.ShapeDtypeStruct((4, rows, width), jnp.float32)
    scratch = [pltpu.VMEM(src_block.shape, jnp.float32)]
    src_parts = on_tile(push_kernel, (four,) * 4, scratch, high, mid, src_block, mine, other)
    src_parts = list(src_parts)
    came, src_parts[0] = lax.optimization_barrier((came, src_parts[0]))
    tgt_half = on_tile(keep_kernel, half, [], high, mid, src_block, mine, came)
    tgt_sum = scatter_blocks(tgt_half, ("z", "x"), SIDE_GROUPS)
    src_sum = scatter_ring(src_parts[:2], src_parts[2:])
    src_piece = take(src_pot.reshape(-1, rows), y * 2 + a)
    tgt_piece = take(tgt_pot.reshape(-1, rows), (c * NZ + z) * 2 + b)
    return src_piece, tgt_piece, src_sum / total_points, tgt_sum / total_points


def solution(mesh):
    grid = Mesh(mesh.devices.reshape(NZ, NX, NY, NC), ("z", "x", "y", "c"))
    split = ("z", "x", "y", "c")
    return jax.shard_map(
        per_device,
        mesh=grid,
        in_specs=(P(split, None), P(split, None)),
        out_specs=(P(split), P(split), P(split, None), P(split, None)),
        check_vma=False,
    )
```

```python
import math

import jax
import jax.numpy as jnp
from jax import lax
from jax.experimental import pallas as pl
from jax.experimental.pallas import tpu as pltpu
from jax.sharding import Mesh
from jax.sharding import PartitionSpec as P

ITERS = 3
ENTROPY_REG = 0.05
NZ, NX, NY, NC = 8, 4, 8, 2
LANES = 128

A_OF_X = (0, 0, 1, 1)
B_OF_X = (0, 1, 1, 0)
FLIP_A = [(x, NX - 1 - x) for x in range(NX)]
FLIP_B = [(x, x ^ 1) for x in range(NX)]
SWAP = [(0, 1), (1, 0)]
X_OF_AB = {(A_OF_X[x], B_OF_X[x]): x for x in range(NX)}

ROW_GROUPS = [[X_OF_AB[a, b] * NY + y for a in range(2) for y in range(NY)] for b in range(2)]
COL_GROUPS = [
    [(z * NX + X_OF_AB[a, b]) * NC + c for z in range(NZ) for b in range(2) for c in range(NC)]
    for a in range(2)
]

SIDE_GROUPS = [
    [z * NX + X_OF_AB[a, b] for b in range(2) for z in range(NZ)] for a in range(2)
]


def take(buffer, index):
    return lax.dynamic_index_in_dim(buffer, index, 0, keepdims=False)


def all_to_all(blocks, axes, groups):
    return lax.all_to_all(
        blocks, axes, split_axis=0, concat_axis=0, axis_index_groups=groups, tiled=True
    )


PASSES = ((0, 0), (0, 1), (1, 0), (1, 1), (0, 2), (2, 0))
IN_HBM = pl.BlockSpec(memory_space=pltpu.HBM)
WHOLE = pl.BlockSpec(memory_space=pltpu.VMEM)
VMEM_LIMIT = 24 * 1024 * 1024


def scatter_blocks(partial, axes, groups):
    count = len(groups[0])
    blocks = partial.reshape(count, partial.shape[0] // count, partial.shape[1])
    return jnp.sum(all_to_all(blocks, axes, groups), axis=0)


def parts_of(values):
    high = values.astype(jnp.bfloat16)
    rest = values - high.astype(jnp.float32)
    mid = rest.astype(jnp.bfloat16)
    low = (rest - mid.astype(jnp.float32)).astype(jnp.bfloat16)
    return high, mid, low


def product(p, q, contract):
    return lax.dot_general(
        p, q, ((contract[:1], contract[1:]), ((), ())), preferred_element_type=jnp.float32
    )


def three_products(p, q, contract):
    return (
        product(p[0], q[0], contract)
        + product(p[0], q[1], contract)
        + product(p[1], q[0], contract)
    )


def cost_half(left_parts, left_sq, right_ref, cost_ref, place):
    cols, width = right_ref.shape
    right = right_ref[...]
    right_parts = parts_of(right)
    cross = sum(product(left_parts[p][...], right_parts[q], (1, 1)) for p, q in PASSES)
    ones = jnp.ones((8, width), jnp.bfloat16)
    right_sq = sum(product(ones, part, (1, 1)) for part in parts_of(right * right))[:1]
    at = pl.ds(pl.multiple_of(place * cols, LANES), cols)
    cost_ref[:, at] = (left_sq + right_sq - 2.0 * cross) / width


def mine_kernel(*refs):
    pieces, mine_hbm = refs[:2], refs[2]
    src_out, high_ref, mid_ref, low_ref, sq_ref, cost_ref = refs[3:9]
    src_ref, mine_ref, sem, out_sem = refs[9:]
    x, c = (lax.axis_index(name) for name in ("x", "c"))
    a = x // 2
    half = pieces[0].shape[0]
    copies = [pltpu.make_async_copy(mine_hbm, mine_ref, sem.at[2])]
    for side, place in enumerate((a, 1 - a)):
        at = pl.multiple_of(place * half, 8)
        copies.append(
            pltpu.make_async_copy(pieces[side], src_ref.at[pl.ds(at, half)], sem.at[side])
        )
    for copy in copies:
        copy.start()
    for copy in copies:
        copy.wait()
    out = pltpu.make_async_copy(src_ref, src_out, out_sem)
    out.start()
    left = src_ref[...]
    left_sq = jnp.sum(left * left, axis=1, keepdims=True)
    sq_ref[...] = left_sq
    high_ref[...], mid_ref[...], low_ref[...] = parts_of(left)
    cost_half((high_ref, mid_ref, low_ref), left_sq, mine_ref, cost_ref, c)
    out.wait()


def other_kernel(high_ref, mid_ref, low_ref, sq_ref, other_ref, same_ref, cost_ref):
    del same_ref
    place = 1 - lax.axis_index("c")
    cost_half((high_ref, mid_ref, low_ref), sq_ref[...], other_ref, cost_ref, place)


def tile(row_pieces, mine):
    width = mine.shape[1]
    rows, cols = 2 * row_pieces[0].shape[0], 2 * mine.shape[0]
    part = jax.ShapeDtypeStruct((rows, width), jnp.bfloat16)
    src_block, high, mid, low, left_sq, cost = pl.pallas_call(
        mine_kernel,
        out_shape=(
            jax.ShapeDtypeStruct((rows, width), jnp.float32),
            part,
            part,
            part,
            jax.ShapeDtypeStruct((rows, 1), jnp.float32),
            jax.ShapeDtypeStruct((rows, cols), jnp.float32),
        ),
        in_specs=[IN_HBM] * 3,
        out_specs=(IN_HBM,) + (WHOLE,) * 5,
        scratch_shapes=[
            pltpu.VMEM((rows, width), jnp.float32),
            pltpu.VMEM(mine.shape, jnp.float32),
            pltpu.SemaphoreType.DMA((3,)),
            pltpu.SemaphoreType.DMA,
        ],
        compiler_params=pltpu.CompilerParams(vmem_limit_bytes=VMEM_LIMIT),
    )(*row_pieces, mine)
    other = lax.ppermute(mine, "c", SWAP)
    cost = pl.pallas_call(
        other_kernel,
        out_shape=jax.ShapeDtypeStruct((rows, cols), jnp.float32),
        in_specs=[WHOLE] * 6,
        out_specs=WHOLE,
        input_output_aliases={5: 0},
        compiler_params=pltpu.CompilerParams(vmem_limit_bytes=VMEM_LIMIT),
    )(high, mid, low, left_sq, other, cost)
    return src_block, other, cost


def half_of(high_ref, mid_ref, place):
    size = high_ref.shape[1] // 2
    at = pl.ds(pl.multiple_of(place * size, LANES), size)
    return high_ref[:, at], mid_ref[:, at]


def pull(weight_parts, src_ref, tgt):
    pulled = three_products(weight_parts, parts_of(src_ref[...]), (0, 0))
    ones = jnp.ones((src_ref.shape[0], LANES), jnp.bfloat16)
    mass = sum(product(part, ones, (0, 0)) for part in weight_parts)[:, :1]
    return mass * tgt - pulled


def send_kernel(
    src_pot_ref, tgt_pot_ref, cost_ref, src_hbm, other_hbm, sent_ref, high_ref, mid_ref,
    src_ref, tgt_ref, sem,
):
    rows, cols = cost_ref.shape
    copies = (
        pltpu.make_async_copy(src_hbm, src_ref, sem.at[0]),
        pltpu.make_async_copy(other_hbm, tgt_ref, sem.at[1]),
    )
    for copy in copies:
        copy.start()
    lane = lax.broadcasted_iota(jnp.int32, (LANES, LANES), 1)
    sub = lax.broadcasted_iota(jnp.int32, (LANES, LANES), 0)
    for i in range(rows // LANES):
        row = jnp.broadcast_to(src_pot_ref[i : i + 1, :], (LANES, LANES))
        column = jnp.sum(jnp.where(lane == sub, row, 0.0), axis=1, keepdims=True)
        at = slice(i * LANES, (i + 1) * LANES)
        for j in range(cols // LANES):
            to = slice(j * LANES, (j + 1) * LANES)
            total = column + tgt_pot_ref[j : j + 1, :] - cost_ref[at, to]
            weight = jnp.exp(total / ENTROPY_REG)
            high = weight.astype(jnp.bfloat16)
            high_ref[at, to] = high
            mid_ref[at, to] = (weight - high.astype(jnp.float32)).astype(jnp.bfloat16)
    for copy in copies:
        copy.wait()
    place = 1 - lax.axis_index("c")
    sent_ref[...] = pull(half_of(high_ref, mid_ref, place), src_ref, tgt_ref[...])


def part_in_two(values, place, sent_ref, own_ref, part_ref):
    half = own_ref.shape[0]
    part_ref[...] = values
    own_ref[...] = part_ref[pl.ds(pl.multiple_of(place * half, 8), half), :]
    sent_ref[...] = part_ref[pl.ds(pl.multiple_of((1 - place) * half, 8), half), :]


def push_kernel(high_ref, mid_ref, src_ref, mine_ref, other_ref, *out_refs):
    c = lax.axis_index("c")
    a = lax.axis_index("x") // 2
    ones = jnp.ones((mine_ref.shape[0], LANES), jnp.bfloat16)
    pushed, mass = 0.0, 0.0
    for place, ref in ((c, mine_ref), (1 - c, other_ref)):
        weight_parts = half_of(high_ref, mid_ref, place)
        pushed += three_products(weight_parts, parts_of(ref[...]), (1, 0))
        mass += sum(product(part, ones, (1, 0)) for part in weight_parts)
    part_in_two(mass[:, :1] * src_ref[...] - pushed, a, *out_refs)


def keep_kernel(high_ref, mid_ref, src_ref, mine_ref, came_ref, out_ref):
    place = lax.axis_index("c")
    kept = pull(half_of(high_ref, mid_ref, place), src_ref, mine_ref[...])
    out_ref[...] = kept + came_ref[...]


def on_tile(kernel, out_shape, scratch, *args):
    return pl.pallas_call(
        kernel,
        out_shape=out_shape,
        in_specs=[WHOLE] * len(args),
        out_specs=jax.tree.map(lambda _: WHOLE, out_shape),
        scratch_shapes=scratch,
        compiler_params=pltpu.CompilerParams(vmem_limit_bytes=VMEM_LIMIT),
    )(*args)


def exchange(local, axes, groups, count):
    size = local.shape[0]
    flat = local.reshape(1, size // LANES, LANES)
    sent = jnp.broadcast_to(flat, (count, size // LANES, LANES))
    got = all_to_all(sent, axes, groups)
    peak = jnp.max(got, axis=0)
    total = jnp.sum(jnp.exp(got - peak[None]), axis=0)
    return peak + jnp.log(total)


def local_lse(scores, axis):
    peak = jnp.max(scores, axis=axis, keepdims=True)
    total = jnp.sum(jnp.exp(scores - peak), axis=axis)
    return jnp.squeeze(peak, axis) + jnp.log(total)


def per_device(src_emb, tgt_emb):
    rows, width = src_emb.shape
    z, x, y, c = (lax.axis_index(name) for name in ("z", "x", "y", "c"))
    a = x // 2
    b = (x // 2) ^ (x % 2)
    total_points = rows * NZ * NX * NY * NC
    side = lax.all_gather(tgt_emb, "z", axis=0, tiled=True)
    flip = lax.ppermute(side, "x", FLIP_B)
    near = lax.all_gather(src_emb, "y", axis=0, tiled=True)
    far = lax.ppermute(near, "x", FLIP_A)
    mine = jnp.where(b == 0, jnp.concatenate([side, flip]), jnp.concatenate([flip, side]))
    src_block, other, cost = tile((near, far), mine)
    tile_rows, tile_cols = cost.shape
    tgt_pot = jnp.zeros((tile_cols,), jnp.float32)
    log_total = math.log(total_points)
    for _ in range(ITERS):
        lse = local_lse((tgt_pot.reshape(1, tile_cols) - cost) / ENTROPY_REG, 1)
        lse = exchange(lse, ("x", "y"), ROW_GROUPS, 2 * NY)
        src_pot = -ENTROPY_REG * (lse - log_total)
        lse = local_lse((src_pot.reshape(tile_rows, 1) - cost) / ENTROPY_REG, 0)
        lse = exchange(lse, ("z", "x", "c"), COL_GROUPS, 2 * NZ * NC)
        tgt_pot = -ENTROPY_REG * (lse - log_total)
    part = jax.ShapeDtypeStruct(cost.shape, jnp.bfloat16)
    half = jax.ShapeDtypeStruct(mine.shape, jnp.float32)
    sent, high, mid = pl.pallas_call(
        send_kernel,
        out_shape=(half, part, part),
        in_specs=[WHOLE] * 3 + [IN_HBM] * 2,
        out_specs=(WHOLE,) * 3,
        scratch_shapes=[
            pltpu.VMEM(src_block.shape, jnp.float32),
            pltpu.VMEM(mine.shape, jnp.float32),
            pltpu.SemaphoreType.DMA((2,)),
        ],
        compiler_params=pltpu.CompilerParams(vmem_limit_bytes=VMEM_LIMIT),
    )(src_pot, tgt_pot, cost, src_block, other)
    came = lax.ppermute(sent, "c", SWAP)
    quarter = jax.ShapeDtypeStruct(near.shape, jnp.float32)
    scratch = [pltpu.VMEM(src_block.shape, jnp.float32)]
    there, here = on_tile(
        push_kernel, (quarter, quarter), scratch, high, mid, src_block, mine, other
    )
    came, here = lax.optimization_barrier((came, here))
    here = here + lax.ppermute(there, "x", FLIP_A)
    src_sum = lax.psum_scatter(here, "y", scatter_dimension=0, tiled=True)
    tgt_half = on_tile(keep_kernel, half, [], high, mid, src_block, mine, came)
    tgt_sum = scatter_blocks(tgt_half, ("z", "x"), SIDE_GROUPS)
    src_piece = take(src_pot.reshape(-1, rows), a * NY + y)
    tgt_piece = take(tgt_pot.reshape(-1, rows), (c * 2 + b) * NZ + z)
    return src_piece, tgt_piece, src_sum / total_points, tgt_sum / total_points


def solution(mesh):
    grid = Mesh(mesh.devices.reshape(NZ, NX, NY, NC), ("z", "x", "y", "c"))
    split = ("z", "x", "y", "c")
    return jax.shard_map(
        per_device,
        mesh=grid,
        in_specs=(P(split, None), P(split, None)),
        out_specs=(P(split), P(split), P(split, None), P(split, None)),
        check_vma=False,
    )
```

```python
import math

import jax
import jax.numpy as jnp
from jax import lax
from jax.experimental import pallas as pl
from jax.experimental.pallas import tpu as pltpu
from jax.sharding import Mesh
from jax.sharding import PartitionSpec as P

ITERS = 3
ENTROPY_REG = 0.05
NZ, NX, NY, NC = 8, 4, 8, 2
LANES = 128

A_OF_X = (0, 0, 1, 1)
B_OF_X = (0, 1, 1, 0)
FLIP_A = [(x, NX - 1 - x) for x in range(NX)]
FLIP_B = [(x, x ^ 1) for x in range(NX)]
SWAP = [(0, 1), (1, 0)]
X_OF_AB = {(A_OF_X[x], B_OF_X[x]): x for x in range(NX)}

ROW_GROUPS = [[X_OF_AB[a, b] * NY + y for a in range(2) for y in range(NY)] for b in range(2)]
COL_GROUPS = [
    [(z * NX + X_OF_AB[a, b]) * NC + c for z in range(NZ) for b in range(2) for c in range(NC)]
    for a in range(2)
]

SIDE_GROUPS = [
    [z * NX + X_OF_AB[a, b] for b in range(2) for z in range(NZ)] for a in range(2)
]


def take(buffer, index):
    return lax.dynamic_index_in_dim(buffer, index, 0, keepdims=False)


def all_to_all(blocks, axes, groups):
    return lax.all_to_all(
        blocks, axes, split_axis=0, concat_axis=0, axis_index_groups=groups, tiled=True
    )


STEPS = (4, 3, 5, 2, 6, 1, 7)
PASSES = ((0, 0), (0, 1), (1, 0), (1, 1), (0, 2), (2, 0))
IN_HBM = pl.BlockSpec(memory_space=pltpu.HBM)
WHOLE = pl.BlockSpec(memory_space=pltpu.VMEM)
VMEM_LIMIT = 24 * 1024 * 1024


def gather_blocks(shard, axes, groups):
    blocks = jnp.broadcast_to(shard[None], (len(groups[0]),) + shard.shape)
    return all_to_all(blocks, axes, groups).reshape(-1, shard.shape[1])


def scatter_ring(pieces, a):
    total = pieces[-1]
    for k, piece in zip(STEPS, pieces):
        moves = [(i, (i + k) % NY) for i in range(NY)]
        total = total + lax.ppermute(piece, "y", moves)
    return take(total, a) + lax.ppermute(take(total, 1 - a), "x", FLIP_A)


def scatter_blocks(partial, axes, groups):
    count = len(groups[0])
    blocks = partial.reshape(count, partial.shape[0] // count, partial.shape[1])
    return jnp.sum(all_to_all(blocks, axes, groups), axis=0)


def parts_of(values):
    high = values.astype(jnp.bfloat16)
    rest = values - high.astype(jnp.float32)
    mid = rest.astype(jnp.bfloat16)
    low = (rest - mid.astype(jnp.float32)).astype(jnp.bfloat16)
    return high, mid, low


def product(p, q, contract):
    return lax.dot_general(
        p, q, ((contract[:1], contract[1:]), ((), ())), preferred_element_type=jnp.float32
    )


def three_products(p, q, contract):
    return (
        product(p[0], q[0], contract)
        + product(p[0], q[1], contract)
        + product(p[1], q[0], contract)
    )


def cost_half(left_parts, left_sq, right_ref, cost_ref, place):
    cols, width = right_ref.shape
    right = right_ref[...]
    right_parts = parts_of(right)
    cross = sum(product(left_parts[p][...], right_parts[q], (1, 1)) for p, q in PASSES)
    ones = jnp.ones((8, width), jnp.bfloat16)
    right_sq = sum(product(ones, part, (1, 1)) for part in parts_of(right * right))[:1]
    at = pl.ds(pl.multiple_of(place * cols, LANES), cols)
    cost_ref[:, at] = (left_sq + right_sq - 2.0 * cross) / width


def mine_kernel(*refs):
    pieces, mine_hbm = refs[:2], refs[2]
    src_out, high_ref, mid_ref, low_ref, sq_ref, cost_ref = refs[3:9]
    src_ref, mine_ref, sem, out_sem = refs[9:]
    x, c = (lax.axis_index(name) for name in ("x", "c"))
    a = x // 2
    half = pieces[0].shape[0]
    copies = [pltpu.make_async_copy(mine_hbm, mine_ref, sem.at[2])]
    for side, place in enumerate((a, 1 - a)):
        at = pl.multiple_of(place * half, 8)
        copies.append(
            pltpu.make_async_copy(pieces[side], src_ref.at[pl.ds(at, half)], sem.at[side])
        )
    for copy in copies:
        copy.start()
    for copy in copies:
        copy.wait()
    out = pltpu.make_async_copy(src_ref, src_out, out_sem)
    out.start()
    left = src_ref[...]
    left_sq = jnp.sum(left * left, axis=1, keepdims=True)
    sq_ref[...] = left_sq
    high_ref[...], mid_ref[...], low_ref[...] = parts_of(left)
    cost_half((high_ref, mid_ref, low_ref), left_sq, mine_ref, cost_ref, c)
    out.wait()


def other_kernel(high_ref, mid_ref, low_ref, sq_ref, other_ref, same_ref, cost_ref):
    del same_ref
    place = 1 - lax.axis_index("c")
    cost_half((high_ref, mid_ref, low_ref), sq_ref[...], other_ref, cost_ref, place)


def tile(row_pieces, mine):
    width = mine.shape[1]
    rows, cols = 2 * row_pieces[0].shape[0], 2 * mine.shape[0]
    part = jax.ShapeDtypeStruct((rows, width), jnp.bfloat16)
    src_block, high, mid, low, left_sq, cost = pl.pallas_call(
        mine_kernel,
        out_shape=(
            jax.ShapeDtypeStruct((rows, width), jnp.float32),
            part,
            part,
            part,
            jax.ShapeDtypeStruct((rows, 1), jnp.float32),
            jax.ShapeDtypeStruct((rows, cols), jnp.float32),
        ),
        in_specs=[IN_HBM] * 3,
        out_specs=(IN_HBM,) + (WHOLE,) * 5,
        scratch_shapes=[
            pltpu.VMEM((rows, width), jnp.float32),
            pltpu.VMEM(mine.shape, jnp.float32),
            pltpu.SemaphoreType.DMA((3,)),
            pltpu.SemaphoreType.DMA,
        ],
        compiler_params=pltpu.CompilerParams(vmem_limit_bytes=VMEM_LIMIT),
    )(*row_pieces, mine)
    other = lax.ppermute(mine, "c", SWAP)
    cost = pl.pallas_call(
        other_kernel,
        out_shape=jax.ShapeDtypeStruct((rows, cols), jnp.float32),
        in_specs=[WHOLE] * 6,
        out_specs=WHOLE,
        input_output_aliases={5: 0},
        compiler_params=pltpu.CompilerParams(vmem_limit_bytes=VMEM_LIMIT),
    )(high, mid, low, left_sq, other, cost)
    return src_block, other, cost


def half_of(high_ref, mid_ref, place):
    size = high_ref.shape[1] // 2
    at = pl.ds(pl.multiple_of(place * size, LANES), size)
    return high_ref[:, at], mid_ref[:, at]


def pull(weight_parts, src_ref, tgt):
    pulled = three_products(weight_parts, parts_of(src_ref[...]), (0, 0))
    ones = jnp.ones((src_ref.shape[0], LANES), jnp.bfloat16)
    mass = sum(product(part, ones, (0, 0)) for part in weight_parts)[:, :1]
    return mass * tgt - pulled


def send_kernel(
    src_pot_ref, tgt_pot_ref, cost_ref, src_hbm, other_hbm, sent_ref, high_ref, mid_ref,
    src_ref, tgt_ref, sem,
):
    rows, cols = cost_ref.shape
    copies = (
        pltpu.make_async_copy(src_hbm, src_ref, sem.at[0]),
        pltpu.make_async_copy(other_hbm, tgt_ref, sem.at[1]),
    )
    for copy in copies:
        copy.start()
    lane = lax.broadcasted_iota(jnp.int32, (LANES, LANES), 1)
    sub = lax.broadcasted_iota(jnp.int32, (LANES, LANES), 0)
    for i in range(rows // LANES):
        row = jnp.broadcast_to(src_pot_ref[i : i + 1, :], (LANES, LANES))
        column = jnp.sum(jnp.where(lane == sub, row, 0.0), axis=1, keepdims=True)
        at = slice(i * LANES, (i + 1) * LANES)
        for j in range(cols // LANES):
            to = slice(j * LANES, (j + 1) * LANES)
            total = column + tgt_pot_ref[j : j + 1, :] - cost_ref[at, to]
            weight = jnp.exp(total / ENTROPY_REG)
            high = weight.astype(jnp.bfloat16)
            high_ref[at, to] = high
            mid_ref[at, to] = (weight - high.astype(jnp.float32)).astype(jnp.bfloat16)
    for copy in copies:
        copy.wait()
    place = 1 - lax.axis_index("c")
    sent_ref[...] = pull(half_of(high_ref, mid_ref, place), src_ref, tgt_ref[...])


def push_kernel(high_ref, mid_ref, src_ref, mine_ref, other_ref, *out_refs):
    out_refs, part_ref = out_refs[:-1], out_refs[-1]
    y, c = lax.axis_index("y"), lax.axis_index("c")
    ones = jnp.ones((mine_ref.shape[0], LANES), jnp.bfloat16)
    pushed, mass = 0.0, 0.0
    for place, ref in ((c, mine_ref), (1 - c, other_ref)):
        weight_parts = half_of(high_ref, mid_ref, place)
        pushed += three_products(weight_parts, parts_of(ref[...]), (1, 0))
        mass += sum(product(part, ones, (1, 0)) for part in weight_parts)
    part_ref[...] = mass[:, :1] * src_ref[...] - pushed
    size = out_refs[0].shape[1]
    for k, ref in zip(STEPS + (0,), out_refs):
        for a in range(2):
            at = pl.multiple_of((a * NY + (y + k) % NY) * size, 8)
            ref[a] = part_ref[pl.ds(at, size), :]


def keep_kernel(high_ref, mid_ref, src_ref, mine_ref, came_ref, out_ref):
    place = lax.axis_index("c")
    kept = pull(half_of(high_ref, mid_ref, place), src_ref, mine_ref[...])
    out_ref[...] = kept + came_ref[...]


def on_tile(kernel, out_shape, scratch, *args):
    return pl.pallas_call(
        kernel,
        out_shape=out_shape,
        in_specs=[WHOLE] * len(args),
        out_specs=jax.tree.map(lambda _: WHOLE, out_shape),
        scratch_shapes=scratch,
        compiler_params=pltpu.CompilerParams(vmem_limit_bytes=VMEM_LIMIT),
    )(*args)


def exchange(local, axes, groups, count):
    size = local.shape[0]
    flat = local.reshape(1, size // LANES, LANES)
    sent = jnp.broadcast_to(flat, (count, size // LANES, LANES))
    got = all_to_all(sent, axes, groups)
    peak = jnp.max(got, axis=0)
    total = jnp.sum(jnp.exp(got - peak[None]), axis=0)
    return peak + jnp.log(total)


def local_lse(scores, axis):
    peak = jnp.max(scores, axis=axis, keepdims=True)
    total = jnp.sum(jnp.exp(scores - peak), axis=axis)
    return jnp.squeeze(peak, axis) + jnp.log(total)


def per_device(src_emb, tgt_emb):
    rows, width = src_emb.shape
    z, x, y, c = (lax.axis_index(name) for name in ("z", "x", "y", "c"))
    a = x // 2
    b = (x // 2) ^ (x % 2)
    total_points = rows * NZ * NX * NY * NC
    mine = gather_blocks(tgt_emb, ("z", "x"), SIDE_GROUPS)
    near = lax.all_gather(src_emb, "y", axis=0, tiled=True)
    far = lax.ppermute(near, "x", FLIP_A)
    mine, far = lax.optimization_barrier((mine, far))
    src_block, other, cost = tile((near, far), mine)
    tile_rows, tile_cols = cost.shape
    tgt_pot = jnp.zeros((tile_cols,), jnp.float32)
    log_total = math.log(total_points)
    for _ in range(ITERS):
        lse = local_lse((tgt_pot.reshape(1, tile_cols) - cost) / ENTROPY_REG, 1)
        lse = exchange(lse, ("x", "y"), ROW_GROUPS, 2 * NY)
        src_pot = -ENTROPY_REG * (lse - log_total)
        lse = local_lse((src_pot.reshape(tile_rows, 1) - cost) / ENTROPY_REG, 0)
        lse = exchange(lse, ("z", "x", "c"), COL_GROUPS, 2 * NZ * NC)
        tgt_pot = -ENTROPY_REG * (lse - log_total)
    part = jax.ShapeDtypeStruct(cost.shape, jnp.bfloat16)
    half = jax.ShapeDtypeStruct(mine.shape, jnp.float32)
    sent, high, mid = pl.pallas_call(
        send_kernel,
        out_shape=(half, part, part),
        in_specs=[WHOLE] * 3 + [IN_HBM] * 2,
        out_specs=(WHOLE,) * 3,
        scratch_shapes=[
            pltpu.VMEM(src_block.shape, jnp.float32),
            pltpu.VMEM(mine.shape, jnp.float32),
            pltpu.SemaphoreType.DMA((2,)),
        ],
        compiler_params=pltpu.CompilerParams(vmem_limit_bytes=VMEM_LIMIT),
    )(src_pot, tgt_pot, cost, src_block, other)
    came = lax.ppermute(sent, "c", SWAP)
    pair = jax.ShapeDtypeStruct((2, rows, width), jnp.float32)
    scratch = [pltpu.VMEM(src_block.shape, jnp.float32)]
    pieces = on_tile(push_kernel, (pair,) * NY, scratch, high, mid, src_block, mine, other)
    pieces = list(pieces)
    came, pieces[0] = lax.optimization_barrier((came, pieces[0]))
    tgt_half = on_tile(keep_kernel, half, [], high, mid, src_block, mine, came)
    tgt_sum = scatter_blocks(tgt_half, ("z", "x"), SIDE_GROUPS)
    src_sum = scatter_ring(pieces, a)
    src_piece = take(src_pot.reshape(-1, rows), a * NY + y)
    tgt_piece = take(tgt_pot.reshape(-1, rows), (c * 2 + b) * NZ + z)
    return src_piece, tgt_piece, src_sum / total_points, tgt_sum / total_points


def solution(mesh):
    grid = Mesh(mesh.devices.reshape(NZ, NX, NY, NC), ("z", "x", "y", "c"))
    split = ("z", "x", "y", "c")
    return jax.shard_map(
        per_device,
        mesh=grid,
        in_specs=(P(split, None), P(split, None)),
        out_specs=(P(split), P(split), P(split, None), P(split, None)),
        check_vma=False,
    )
```

```python
import math

import jax
import jax.numpy as jnp
from jax import lax
from jax.experimental import pallas as pl
from jax.experimental.pallas import tpu as pltpu
from jax.sharding import Mesh
from jax.sharding import PartitionSpec as P

ITERS = 3
ENTROPY_REG = 0.05
NZ, NX, NY, NC = 8, 4, 8, 2
LANES = 128

A_OF_X = (0, 0, 1, 1)
B_OF_X = (0, 1, 1, 0)
FLIP_A = [(x, NX - 1 - x) for x in range(NX)]
FLIP_B = [(x, x ^ 1) for x in range(NX)]
SWAP = [(0, 1), (1, 0)]
X_OF_AB = {(A_OF_X[x], B_OF_X[x]): x for x in range(NX)}

ROW_GROUPS = [[X_OF_AB[a, b] * NY + y for a in range(2) for y in range(NY)] for b in range(2)]
COL_GROUPS = [
    [(z * NX + X_OF_AB[a, b]) * NC + c for z in range(NZ) for b in range(2) for c in range(NC)]
    for a in range(2)
]

SIDE_GROUPS = [
    [z * NX + X_OF_AB[a, b] for b in range(2) for z in range(NZ)] for a in range(2)
]


def take(buffer, index):
    return lax.dynamic_index_in_dim(buffer, index, 0, keepdims=False)


def all_to_all(blocks, axes, groups):
    return lax.all_to_all(
        blocks, axes, split_axis=0, concat_axis=0, axis_index_groups=groups, tiled=True
    )


STEPS = (4, 3, 5, 2, 6, 1, 7)
PASSES = ((0, 0), (0, 1), (1, 0), (1, 1), (0, 2), (2, 0))
IN_HBM = pl.BlockSpec(memory_space=pltpu.HBM)
WHOLE = pl.BlockSpec(memory_space=pltpu.VMEM)
VMEM_LIMIT = 24 * 1024 * 1024


def gather_blocks(shard, axes, groups):
    blocks = jnp.broadcast_to(shard[None], (len(groups[0]),) + shard.shape)
    return all_to_all(blocks, axes, groups).reshape(-1, shard.shape[1])


def scatter_ring(pieces, a):
    total = pieces[-1]
    for k, piece in zip(STEPS, pieces):
        moves = [(i, (i + k) % NY) for i in range(NY)]
        total = total + lax.ppermute(piece, "y", moves)
    return take(total, a) + lax.ppermute(take(total, 1 - a), "x", FLIP_A)


def scatter_blocks(partial, axes, groups):
    count = len(groups[0])
    blocks = partial.reshape(count, partial.shape[0] // count, partial.shape[1])
    return jnp.sum(all_to_all(blocks, axes, groups), axis=0)


def parts_of(values):
    high = values.astype(jnp.bfloat16)
    rest = values - high.astype(jnp.float32)
    mid = rest.astype(jnp.bfloat16)
    low = (rest - mid.astype(jnp.float32)).astype(jnp.bfloat16)
    return high, mid, low


def product(p, q, contract):
    return lax.dot_general(
        p, q, ((contract[:1], contract[1:]), ((), ())), preferred_element_type=jnp.float32
    )


def three_products(p, q, contract):
    return (
        product(p[0], q[0], contract)
        + product(p[0], q[1], contract)
        + product(p[1], q[0], contract)
    )


def cost_half(left_parts, left_sq, right_ref, cost_ref, place):
    cols, width = right_ref.shape
    right = right_ref[...]
    right_parts = parts_of(right)
    cross = sum(product(left_parts[p][...], right_parts[q], (1, 1)) for p, q in PASSES)
    ones = jnp.ones((8, width), jnp.bfloat16)
    right_sq = sum(product(ones, part, (1, 1)) for part in parts_of(right * right))[:1]
    at = pl.ds(pl.multiple_of(place * cols, LANES), cols)
    cost_ref[:, at] = (left_sq + right_sq - 2.0 * cross) / width


def mine_kernel(*refs):
    pieces, mine_hbm = refs[:2], refs[2]
    src_out, high_ref, mid_ref, low_ref, sq_ref, cost_ref = refs[3:9]
    src_ref, mine_ref, sem, out_sem = refs[9:]
    x, c = (lax.axis_index(name) for name in ("x", "c"))
    a = x // 2
    half = pieces[0].shape[0]
    copies = [pltpu.make_async_copy(mine_hbm, mine_ref, sem.at[2])]
    for side, place in enumerate((a, 1 - a)):
        at = pl.multiple_of(place * half, 8)
        copies.append(
            pltpu.make_async_copy(pieces[side], src_ref.at[pl.ds(at, half)], sem.at[side])
        )
    for copy in copies:
        copy.start()
    for copy in copies:
        copy.wait()
    out = pltpu.make_async_copy(src_ref, src_out, out_sem)
    out.start()
    left = src_ref[...]
    left_sq = jnp.sum(left * left, axis=1, keepdims=True)
    sq_ref[...] = left_sq
    high_ref[...], mid_ref[...], low_ref[...] = parts_of(left)
    cost_half((high_ref, mid_ref, low_ref), left_sq, mine_ref, cost_ref, c)
    out.wait()


def other_kernel(high_ref, mid_ref, low_ref, sq_ref, other_ref, same_ref, cost_ref):
    del same_ref
    place = 1 - lax.axis_index("c")
    cost_half((high_ref, mid_ref, low_ref), sq_ref[...], other_ref, cost_ref, place)


def tile(row_pieces, mine):
    width = mine.shape[1]
    rows, cols = 2 * row_pieces[0].shape[0], 2 * mine.shape[0]
    part = jax.ShapeDtypeStruct((rows, width), jnp.bfloat16)
    src_block, high, mid, low, left_sq, cost = pl.pallas_call(
        mine_kernel,
        out_shape=(
            jax.ShapeDtypeStruct((rows, width), jnp.float32),
            part,
            part,
            part,
            jax.ShapeDtypeStruct((rows, 1), jnp.float32),
            jax.ShapeDtypeStruct((rows, cols), jnp.float32),
        ),
        in_specs=[IN_HBM] * 3,
        out_specs=(IN_HBM,) + (WHOLE,) * 5,
        scratch_shapes=[
            pltpu.VMEM((rows, width), jnp.float32),
            pltpu.VMEM(mine.shape, jnp.float32),
            pltpu.SemaphoreType.DMA((3,)),
            pltpu.SemaphoreType.DMA,
        ],
        compiler_params=pltpu.CompilerParams(vmem_limit_bytes=VMEM_LIMIT),
    )(*row_pieces, mine)
    other = lax.ppermute(mine, "c", SWAP)
    cost = pl.pallas_call(
        other_kernel,
        out_shape=jax.ShapeDtypeStruct((rows, cols), jnp.float32),
        in_specs=[WHOLE] * 6,
        out_specs=WHOLE,
        input_output_aliases={5: 0},
        compiler_params=pltpu.CompilerParams(vmem_limit_bytes=VMEM_LIMIT),
    )(high, mid, low, left_sq, other, cost)
    return src_block, other, cost


def half_of(high_ref, mid_ref, place):
    size = high_ref.shape[1] // 2
    at = pl.ds(pl.multiple_of(place * size, LANES), size)
    return high_ref[:, at], mid_ref[:, at]


def pull(weight_parts, src_ref, tgt):
    pulled = three_products(weight_parts, parts_of(src_ref[...]), (0, 0))
    ones = jnp.ones((src_ref.shape[0], LANES), jnp.bfloat16)
    mass = sum(product(part, ones, (0, 0)) for part in weight_parts)[:, :1]
    return mass * tgt - pulled


def columns_of(row):
    lane = lax.broadcasted_iota(jnp.int32, (LANES, LANES), 1)
    sub = lax.broadcasted_iota(jnp.int32, (LANES, LANES), 0)
    square = jnp.where(lane == sub, jnp.broadcast_to(row, (LANES, LANES)), 0.0)
    return jnp.sum(square, axis=1, keepdims=True)


def weight_kernel(src_pot_ref, tgt_pot_ref, cost_ref, high_ref, mid_ref, sum_ref):
    rows, cols = cost_ref.shape
    sums = [0.0] * (cols // LANES)
    for i in range(rows // LANES):
        column = columns_of(src_pot_ref[i : i + 1, :])
        at = slice(i * LANES, (i + 1) * LANES)
        for j in range(cols // LANES):
            to = slice(j * LANES, (j + 1) * LANES)
            total = column + tgt_pot_ref[j : j + 1, :] - cost_ref[at, to]
            weight = jnp.exp(total / ENTROPY_REG)
            high = weight.astype(jnp.bfloat16)
            high_ref[at, to] = high
            mid_ref[at, to] = (weight - high.astype(jnp.float32)).astype(jnp.bfloat16)
            sums[j] += jnp.sum(weight, axis=0, keepdims=True)
    for j, value in enumerate(sums):
        sum_ref[j : j + 1, :] = value


def send_kernel(high_ref, mid_ref, src_ref, other_ref, sent_ref):
    place = 1 - lax.axis_index("c")
    sent_ref[...] = pull(half_of(high_ref, mid_ref, place), src_ref, other_ref[...])


def push_kernel(high_ref, mid_ref, scale_ref, src_ref, mine_ref, other_ref, *out_refs):
    out_refs, (part_ref, tgt_ref, wide_ref) = out_refs[:-3], out_refs[-3:]
    y, c = lax.axis_index("y"), lax.axis_index("c")
    count = scale_ref.shape[0] // 2
    pushed, mass = 0.0, 0.0
    for place, ref in ((c, mine_ref), (1 - c, other_ref)):
        for i in range(count):
            low, high = scale_ref[i : i + 1, :], scale_ref[count + i : count + i + 1, :]
            column = columns_of(jnp.where(place == 0, low, high))
            at = slice(i * LANES, (i + 1) * LANES)
            tgt_ref[at, :] = ref[at, :] * column
            wide_ref[at, :] = jnp.broadcast_to(column, (LANES, LANES))
        weight_parts = half_of(high_ref, mid_ref, place)
        pushed += three_products(weight_parts, parts_of(tgt_ref[...]), (1, 0))
        mass += three_products(weight_parts, parts_of(wide_ref[...]), (1, 0))
    part_ref[...] = mass[:, :1] * src_ref[...] - pushed
    size = out_refs[0].shape[1]
    for k, ref in zip(STEPS + (0,), out_refs):
        for a in range(2):
            at = pl.multiple_of((a * NY + (y + k) % NY) * size, 8)
            ref[a] = part_ref[pl.ds(at, size), :]


def keep_kernel(high_ref, mid_ref, src_ref, mine_ref, came_ref, out_ref):
    place = lax.axis_index("c")
    kept = pull(half_of(high_ref, mid_ref, place), src_ref, mine_ref[...])
    out_ref[...] = kept + came_ref[...]


def on_tile(kernel, out_shape, scratch, *args):
    return pl.pallas_call(
        kernel,
        out_shape=out_shape,
        in_specs=[WHOLE] * len(args),
        out_specs=jax.tree.map(lambda _: WHOLE, out_shape),
        scratch_shapes=scratch,
        compiler_params=pltpu.CompilerParams(vmem_limit_bytes=VMEM_LIMIT),
    )(*args)


def gather_lanes(local, axes, groups):
    count = len(groups[0])
    flat = local.reshape(1, local.size // LANES, LANES)
    return all_to_all(jnp.broadcast_to(flat, (count,) + flat.shape[1:]), axes, groups)


def exchange(local, axes, groups):
    got = gather_lanes(local, axes, groups)
    peak = jnp.max(got, axis=0)
    total = jnp.sum(jnp.exp(got - peak[None]), axis=0)
    return peak + jnp.log(total)


def local_lse(scores, axis):
    peak = jnp.max(scores, axis=axis, keepdims=True)
    total = jnp.sum(jnp.exp(scores - peak), axis=axis)
    return jnp.squeeze(peak, axis) + jnp.log(total)


def per_device(src_emb, tgt_emb):
    rows, width = src_emb.shape
    z, x, y, c = (lax.axis_index(name) for name in ("z", "x", "y", "c"))
    a = x // 2
    b = (x // 2) ^ (x % 2)
    total_points = rows * NZ * NX * NY * NC
    mine = gather_blocks(tgt_emb, ("z", "x"), SIDE_GROUPS)
    near = lax.all_gather(src_emb, "y", axis=0, tiled=True)
    far = lax.ppermute(near, "x", FLIP_A)
    mine, far = lax.optimization_barrier((mine, far))
    src_block, other, cost = tile((near, far), mine)
    tile_rows, tile_cols = cost.shape
    log_total = math.log(total_points)
    row_axes, col_axes = ("x", "y"), ("z", "x", "c")
    lse = exchange(local_lse(-cost / ENTROPY_REG, 1), row_axes, ROW_GROUPS)
    src_pot = -ENTROPY_REG * (lse - log_total)
    scores = (src_pot.reshape(tile_rows, 1) - cost) / ENTROPY_REG
    lse = exchange(local_lse(scores, 0), col_axes, COL_GROUPS)
    tgt_pot = -ENTROPY_REG * (lse - log_total)

    def weights():
        total = src_pot.reshape(tile_rows, 1) + tgt_pot.reshape(1, tile_cols) - cost
        return jnp.exp(total / ENTROPY_REG)

    for iteration in range(1, ITERS):
        row_sums = gather_lanes(jnp.sum(weights(), axis=1), row_axes, ROW_GROUPS)
        row_sums = jnp.sum(row_sums, axis=0)
        src_pot = src_pot - ENTROPY_REG * (jnp.log(row_sums) - log_total)
        if iteration < ITERS - 1:
            col_sums = gather_lanes(jnp.sum(weights(), axis=0), col_axes, COL_GROUPS)
            col_sums = jnp.sum(col_sums, axis=0)
            tgt_pot = tgt_pot - ENTROPY_REG * (jnp.log(col_sums) - log_total)
    part = jax.ShapeDtypeStruct(cost.shape, jnp.bfloat16)
    half = jax.ShapeDtypeStruct(mine.shape, jnp.float32)
    lanes = jax.ShapeDtypeStruct(tgt_pot.shape, jnp.float32)
    high, mid, col_sums = on_tile(
        weight_kernel, (part, part, lanes), [], src_pot, tgt_pot, cost
    )
    col_sums = gather_lanes(col_sums, col_axes, COL_GROUPS)
    sent = on_tile(send_kernel, half, [], high, mid, src_block, other)
    came = lax.ppermute(sent, "c", SWAP)
    tgt_half = on_tile(keep_kernel, half, [], high, mid, src_block, mine, came)
    tgt_half, col_sums = lax.optimization_barrier((tgt_half, col_sums))
    tgt_sum = scatter_blocks(tgt_half, ("z", "x"), SIDE_GROUPS)
    col_sums = jnp.sum(col_sums, axis=0)
    tgt_pot = tgt_pot - ENTROPY_REG * (jnp.log(col_sums) - log_total)
    pair = jax.ShapeDtypeStruct((2, rows, width), jnp.float32)
    scratch = [
        pltpu.VMEM(src_block.shape, jnp.float32),
        pltpu.VMEM(mine.shape, jnp.float32),
        pltpu.VMEM((mine.shape[0], LANES), jnp.float32),
    ]
    pieces = on_tile(
        push_kernel, (pair,) * NY, scratch,
        high, mid, total_points / col_sums, src_block, mine, other,
    )
    src_sum = scatter_ring(pieces, a)
    src_piece = take(src_pot.reshape(-1, rows), a * NY + y)
    tgt_piece = take(tgt_pot.reshape(-1, rows), (c * 2 + b) * NZ + z)
    col_sum = take(col_sums.reshape(-1, rows), (c * 2 + b) * NZ + z)
    return src_piece, tgt_piece, src_sum / total_points, tgt_sum / col_sum[:, None]


def solution(mesh):
    grid = Mesh(mesh.devices.reshape(NZ, NX, NY, NC), ("z", "x", "y", "c"))
    split = ("z", "x", "y", "c")
    return jax.shard_map(
        per_device,
        mesh=grid,
        in_specs=(P(split, None), P(split, None)),
        out_specs=(P(split), P(split), P(split, None), P(split, None)),
        check_vma=False,
    )
```

```python
import math

import jax
import jax.numpy as jnp
from jax import lax
from jax.experimental import pallas as pl
from jax.experimental.pallas import tpu as pltpu
from jax.sharding import Mesh
from jax.sharding import PartitionSpec as P

ITERS = 3
ENTROPY_REG = 0.05
NZ, NX, NY, NC = 8, 4, 8, 2
LANES = 128

A_OF_X = (0, 0, 1, 1)
B_OF_X = (0, 1, 1, 0)
FLIP_A = [(x, NX - 1 - x) for x in range(NX)]
FLIP_B = [(x, x ^ 1) for x in range(NX)]
SWAP = [(0, 1), (1, 0)]
X_OF_AB = {(A_OF_X[x], B_OF_X[x]): x for x in range(NX)}

ROW_GROUPS = [[X_OF_AB[a, b] * NY + y for a in range(2) for y in range(NY)] for b in range(2)]
COL_GROUPS = [
    [(z * NX + X_OF_AB[a, b]) * NC + c for z in range(NZ) for b in range(2) for c in range(NC)]
    for a in range(2)
]

SIDE_GROUPS = [
    [z * NX + X_OF_AB[a, b] for b in range(2) for z in range(NZ)] for a in range(2)
]


def take(buffer, index):
    return lax.dynamic_index_in_dim(buffer, index, 0, keepdims=False)


def all_to_all(blocks, axes, groups):
    return lax.all_to_all(
        blocks, axes, split_axis=0, concat_axis=0, axis_index_groups=groups, tiled=True
    )


STEPS = (4, 3, 5, 2, 6, 1, 7)
PASSES = ((0, 0), (0, 1), (1, 0), (1, 1), (0, 2), (2, 0))
IN_HBM = pl.BlockSpec(memory_space=pltpu.HBM)
WHOLE = pl.BlockSpec(memory_space=pltpu.VMEM)
VMEM_LIMIT = 24 * 1024 * 1024


def gather_blocks(shard, axes, groups):
    blocks = jnp.broadcast_to(shard[None], (len(groups[0]),) + shard.shape)
    return all_to_all(blocks, axes, groups).reshape(-1, shard.shape[1])


def sum_pieces(pieces, b):
    total = sum(pieces)
    return take(total, b) + lax.ppermute(take(total, 1 - b), "x", FLIP_B)


def scatter_blocks(partial, axes, groups):
    count = len(groups[0])
    blocks = partial.reshape(count, partial.shape[0] // count, partial.shape[1])
    return jnp.sum(all_to_all(blocks, axes, groups), axis=0)


def parts_of(values):
    high = values.astype(jnp.bfloat16)
    rest = values - high.astype(jnp.float32)
    mid = rest.astype(jnp.bfloat16)
    low = (rest - mid.astype(jnp.float32)).astype(jnp.bfloat16)
    return high, mid, low


def product(p, q, contract):
    return lax.dot_general(
        p, q, ((contract[:1], contract[1:]), ((), ())), preferred_element_type=jnp.float32
    )


def three_products(p, q, contract):
    return (
        product(p[0], q[0], contract)
        + product(p[0], q[1], contract)
        + product(p[1], q[0], contract)
    )


def cost_half(left_parts, left_sq, right_ref, cost_ref, place):
    cols, width = right_ref.shape
    right = right_ref[...]
    right_parts = parts_of(right)
    cross = sum(product(left_parts[p][...], right_parts[q], (1, 1)) for p, q in PASSES)
    ones = jnp.ones((8, width), jnp.bfloat16)
    right_sq = sum(product(ones, part, (1, 1)) for part in parts_of(right * right))[:1]
    at = pl.ds(pl.multiple_of(place * cols, LANES), cols)
    cost_ref[:, at] = (left_sq + right_sq - 2.0 * cross) / width


def mine_kernel(*refs):
    pieces, mine_hbm = refs[:2], refs[2]
    src_out, high_ref, mid_ref, low_ref, sq_ref, cost_ref = refs[3:9]
    src_ref, mine_ref, sem, out_sem = refs[9:]
    x, c = (lax.axis_index(name) for name in ("x", "c"))
    a = x // 2
    half = pieces[0].shape[0]
    copies = [pltpu.make_async_copy(mine_hbm, mine_ref, sem.at[2])]
    for side, place in enumerate((a, 1 - a)):
        at = pl.multiple_of(place * half, 8)
        copies.append(
            pltpu.make_async_copy(pieces[side], src_ref.at[pl.ds(at, half)], sem.at[side])
        )
    for copy in copies:
        copy.start()
    for copy in copies:
        copy.wait()
    out = pltpu.make_async_copy(src_ref, src_out, out_sem)
    out.start()
    left = src_ref[...]
    left_sq = jnp.sum(left * left, axis=1, keepdims=True)
    sq_ref[...] = left_sq
    high_ref[...], mid_ref[...], low_ref[...] = parts_of(left)
    cost_half((high_ref, mid_ref, low_ref), left_sq, mine_ref, cost_ref, c)
    out.wait()


def other_kernel(high_ref, mid_ref, low_ref, sq_ref, other_ref, same_ref, cost_ref):
    del same_ref
    place = 1 - lax.axis_index("c")
    cost_half((high_ref, mid_ref, low_ref), sq_ref[...], other_ref, cost_ref, place)


def tile(row_pieces, mine):
    width = mine.shape[1]
    rows, cols = 2 * row_pieces[0].shape[0], 2 * mine.shape[0]
    part = jax.ShapeDtypeStruct((rows, width), jnp.bfloat16)
    src_block, high, mid, low, left_sq, cost = pl.pallas_call(
        mine_kernel,
        out_shape=(
            jax.ShapeDtypeStruct((rows, width), jnp.float32),
            part,
            part,
            part,
            jax.ShapeDtypeStruct((rows, 1), jnp.float32),
            jax.ShapeDtypeStruct((rows, cols), jnp.float32),
        ),
        in_specs=[IN_HBM] * 3,
        out_specs=(IN_HBM,) + (WHOLE,) * 5,
        scratch_shapes=[
            pltpu.VMEM((rows, width), jnp.float32),
            pltpu.VMEM(mine.shape, jnp.float32),
            pltpu.SemaphoreType.DMA((3,)),
            pltpu.SemaphoreType.DMA,
        ],
        compiler_params=pltpu.CompilerParams(vmem_limit_bytes=VMEM_LIMIT),
    )(*row_pieces, mine)
    other = lax.ppermute(mine, "c", SWAP)
    cost = pl.pallas_call(
        other_kernel,
        out_shape=jax.ShapeDtypeStruct((rows, cols), jnp.float32),
        in_specs=[WHOLE] * 6,
        out_specs=WHOLE,
        input_output_aliases={5: 0},
        compiler_params=pltpu.CompilerParams(vmem_limit_bytes=VMEM_LIMIT),
    )(high, mid, low, left_sq, other, cost)
    return src_block, other, cost


def half_of(high_ref, mid_ref, place):
    size = high_ref.shape[1] // 2
    at = pl.ds(pl.multiple_of(place * size, LANES), size)
    return high_ref[:, at], mid_ref[:, at]


def pull(weight_parts, src_ref, tgt):
    pulled = three_products(weight_parts, parts_of(src_ref[...]), (0, 0))
    ones = jnp.ones((src_ref.shape[0], LANES), jnp.bfloat16)
    mass = sum(product(part, ones, (0, 0)) for part in weight_parts)[:, :1]
    return mass * tgt - pulled


def columns_of(row):
    lane = lax.broadcasted_iota(jnp.int32, (LANES, LANES), 1)
    sub = lax.broadcasted_iota(jnp.int32, (LANES, LANES), 0)
    square = jnp.where(lane == sub, jnp.broadcast_to(row, (LANES, LANES)), 0.0)
    return jnp.sum(square, axis=1, keepdims=True)


def weight_kernel(src_pot_ref, tgt_pot_ref, cost_ref, high_ref, mid_ref, sum_ref):
    rows, cols = cost_ref.shape
    sums = [0.0] * (cols // LANES)
    for i in range(rows // LANES):
        column = columns_of(src_pot_ref[i : i + 1, :])
        at = slice(i * LANES, (i + 1) * LANES)
        for j in range(cols // LANES):
            to = slice(j * LANES, (j + 1) * LANES)
            total = column + tgt_pot_ref[j : j + 1, :] - cost_ref[at, to]
            weight = jnp.exp(total / ENTROPY_REG)
            high = weight.astype(jnp.bfloat16)
            high_ref[at, to] = high
            mid_ref[at, to] = (weight - high.astype(jnp.float32)).astype(jnp.bfloat16)
            sums[j] += jnp.sum(weight, axis=0, keepdims=True)
    for j, value in enumerate(sums):
        sum_ref[j : j + 1, :] = value


def pull_kernel(high_ref, mid_ref, src_ref, mine_ref, other_ref, sent_ref, kept_ref):
    c = lax.axis_index("c")
    sent_ref[...] = pull(half_of(high_ref, mid_ref, 1 - c), src_ref, other_ref[...])
    kept_ref[...] = pull(half_of(high_ref, mid_ref, c), src_ref, mine_ref[...])


def order_kernel(kept_ref, came_ref, *out_refs):
    z = lax.axis_index("z")
    size = out_refs[0].shape[1]
    for k, ref in zip(STEPS + (0,), out_refs):
        for b in range(2):
            at = pl.ds(pl.multiple_of((b * NZ + (z + k) % NZ) * size, 8), size)
            ref[b] = kept_ref[at, :] + came_ref[at, :]


def push_kernel(high_ref, mid_ref, scale_ref, src_ref, mine_ref, other_ref, *out_refs):
    out_ref, tgt_ref, wide_ref = out_refs
    c = lax.axis_index("c")
    count = scale_ref.shape[0] // 2
    pushed, mass = 0.0, 0.0
    for place, ref in ((c, mine_ref), (1 - c, other_ref)):
        for i in range(count):
            low, high = scale_ref[i : i + 1, :], scale_ref[count + i : count + i + 1, :]
            column = columns_of(jnp.where(place == 0, low, high))
            at = slice(i * LANES, (i + 1) * LANES)
            tgt_ref[at, :] = ref[at, :] * column
            wide_ref[at, :] = jnp.broadcast_to(column, (LANES, LANES))
        weight_parts = half_of(high_ref, mid_ref, place)
        pushed += three_products(weight_parts, parts_of(tgt_ref[...]), (1, 0))
        mass += three_products(weight_parts, parts_of(wide_ref[...]), (1, 0))
    out_ref[...] = mass[:, :1] * src_ref[...] - pushed


def on_tile(kernel, out_shape, scratch, *args):
    return pl.pallas_call(
        kernel,
        out_shape=out_shape,
        in_specs=[WHOLE] * len(args),
        out_specs=jax.tree.map(lambda _: WHOLE, out_shape),
        scratch_shapes=scratch,
        compiler_params=pltpu.CompilerParams(vmem_limit_bytes=VMEM_LIMIT),
    )(*args)


def gather_lanes(local, axes, groups):
    count = len(groups[0])
    flat = local.reshape(1, local.size // LANES, LANES)
    return all_to_all(jnp.broadcast_to(flat, (count,) + flat.shape[1:]), axes, groups)


def exchange(local, axes, groups):
    got = gather_lanes(local, axes, groups)
    peak = jnp.max(got, axis=0)
    total = jnp.sum(jnp.exp(got - peak[None]), axis=0)
    return peak + jnp.log(total)


def local_lse(scores, axis):
    peak = jnp.max(scores, axis=axis, keepdims=True)
    total = jnp.sum(jnp.exp(scores - peak), axis=axis)
    return jnp.squeeze(peak, axis) + jnp.log(total)


def per_device(src_emb, tgt_emb):
    rows, width = src_emb.shape
    z, x, y, c = (lax.axis_index(name) for name in ("z", "x", "y", "c"))
    a = x // 2
    b = (x // 2) ^ (x % 2)
    total_points = rows * NZ * NX * NY * NC
    mine = gather_blocks(tgt_emb, ("z", "x"), SIDE_GROUPS)
    near = lax.all_gather(src_emb, "y", axis=0, tiled=True)
    far = lax.ppermute(near, "x", FLIP_A)
    mine, far = lax.optimization_barrier((mine, far))
    src_block, other, cost = tile((near, far), mine)
    tile_rows, tile_cols = cost.shape
    log_total = math.log(total_points)
    row_axes, col_axes = ("x", "y"), ("z", "x", "c")
    tgt_pot = jnp.zeros((tile_cols,), jnp.float32)
    for iteration in range(ITERS):
        scores = (tgt_pot.reshape(1, tile_cols) - cost) / ENTROPY_REG
        lse = exchange(local_lse(scores, 1), row_axes, ROW_GROUPS)
        src_pot = -ENTROPY_REG * (lse - log_total)
        if iteration < ITERS - 1:
            scores = (src_pot.reshape(tile_rows, 1) - cost) / ENTROPY_REG
            lse = exchange(local_lse(scores, 0), col_axes, COL_GROUPS)
            tgt_pot = -ENTROPY_REG * (lse - log_total)

    part = jax.ShapeDtypeStruct(cost.shape, jnp.bfloat16)
    half = jax.ShapeDtypeStruct(mine.shape, jnp.float32)
    lanes = jax.ShapeDtypeStruct(tgt_pot.shape, jnp.float32)
    high, mid, col_sums = on_tile(
        weight_kernel, (part, part, lanes), [], src_pot, tgt_pot, cost
    )
    col_sums = gather_lanes(col_sums, col_axes, COL_GROUPS)
    sent, kept = on_tile(
        pull_kernel, (half, half), [], high, mid, src_block, mine, other
    )
    came = lax.ppermute(sent, "c", SWAP)
    pair = jax.ShapeDtypeStruct((2, rows, width), jnp.float32)
    pieces = list(on_tile(order_kernel, (pair,) * NZ, [], kept, came))
    for i, k in enumerate(STEPS):
        moves = [(place, (place + k) % NZ) for place in range(NZ)]
        pieces[i] = lax.ppermute(pieces[i], "z", moves)
    pieces[0], col_sums = lax.optimization_barrier((pieces[0], col_sums))
    tgt_sum = sum_pieces(pieces, b)
    col_sums = jnp.sum(col_sums, axis=0)
    tgt_pot = tgt_pot - ENTROPY_REG * (jnp.log(col_sums) - log_total)
    block = jax.ShapeDtypeStruct(src_block.shape, jnp.float32)
    scratch = [
        pltpu.VMEM(mine.shape, jnp.float32),
        pltpu.VMEM((mine.shape[0], LANES), jnp.float32),
    ]
    src_part = on_tile(
        push_kernel, block, scratch,
        high, mid, total_points / col_sums, src_block, mine, other,
    )
    src_sum = scatter_blocks(src_part, row_axes, ROW_GROUPS)
    src_piece = take(src_pot.reshape(-1, rows), a * NY + y)
    tgt_piece = take(tgt_pot.reshape(-1, rows), (c * 2 + b) * NZ + z)
    col_sum = take(col_sums.reshape(-1, rows), (c * 2 + b) * NZ + z)
    return src_piece, tgt_piece, src_sum / total_points, tgt_sum / col_sum[:, None]


def solution(mesh):
    grid = Mesh(mesh.devices.reshape(NZ, NX, NY, NC), ("z", "x", "y", "c"))
    split = ("z", "x", "y", "c")
    return jax.shard_map(
        per_device,
        mesh=grid,
        in_specs=(P(split, None), P(split, None)),
        out_specs=(P(split), P(split), P(split, None), P(split, None)),
        check_vma=False,
    )
```

```python
import math

import jax
import jax.numpy as jnp
from jax import lax
from jax.experimental import pallas as pl
from jax.experimental.pallas import tpu as pltpu
from jax.sharding import Mesh
from jax.sharding import PartitionSpec as P

ITERS = 3
ENTROPY_REG = 0.05
NZ, NX, NY, NC = 8, 4, 8, 2
LANES = 128

A_OF_X = (0, 0, 1, 1)
B_OF_X = (0, 1, 1, 0)
FLIP_A = [(x, NX - 1 - x) for x in range(NX)]
FLIP_B = [(x, x ^ 1) for x in range(NX)]
SWAP = [(0, 1), (1, 0)]
X_OF_AB = {(A_OF_X[x], B_OF_X[x]): x for x in range(NX)}

ROW_GROUPS = [[X_OF_AB[a, b] * NY + y for a in range(2) for y in range(NY)] for b in range(2)]
COL_GROUPS = [
    [(z * NX + X_OF_AB[a, b]) * NC + c for z in range(NZ) for b in range(2) for c in range(NC)]
    for a in range(2)
]

SIDE_GROUPS = [
    [z * NX + X_OF_AB[a, b] for b in range(2) for z in range(NZ)] for a in range(2)
]


def take(buffer, index):
    return lax.dynamic_index_in_dim(buffer, index, 0, keepdims=False)


def all_to_all(blocks, axes, groups):
    return lax.all_to_all(
        blocks, axes, split_axis=0, concat_axis=0, axis_index_groups=groups, tiled=True
    )


STEPS = (4, 3, 5, 2, 6, 1, 7)
PASSES = ((0, 0), (0, 1), (1, 0), (1, 1), (0, 2), (2, 0))
IN_HBM = pl.BlockSpec(memory_space=pltpu.HBM)
WHOLE = pl.BlockSpec(memory_space=pltpu.VMEM)
VMEM_LIMIT = 24 * 1024 * 1024


def gather_blocks(shard, axes, groups):
    blocks = jnp.broadcast_to(shard[None], (len(groups[0]),) + shard.shape)
    return all_to_all(blocks, axes, groups).reshape(-1, shard.shape[1])


def scatter_ring(pieces, a):
    total = pieces[-1]
    for k, piece in zip(STEPS, pieces):
        moves = [(i, (i + k) % NY) for i in range(NY)]
        total = total + lax.ppermute(piece, "y", moves)
    return take(total, a) + lax.ppermute(take(total, 1 - a), "x", FLIP_A)


def scatter_blocks(partial, axes, groups):
    count = len(groups[0])
    blocks = partial.reshape(count, partial.shape[0] // count, partial.shape[1])
    return jnp.sum(all_to_all(blocks, axes, groups), axis=0)


def parts_of(values):
    high = values.astype(jnp.bfloat16)
    rest = values - high.astype(jnp.float32)
    mid = rest.astype(jnp.bfloat16)
    low = (rest - mid.astype(jnp.float32)).astype(jnp.bfloat16)
    return high, mid, low


def product(p, q, contract):
    return lax.dot_general(
        p, q, ((contract[:1], contract[1:]), ((), ())), preferred_element_type=jnp.float32
    )


def three_products(p, q, contract):
    return (
        product(p[0], q[0], contract)
        + product(p[0], q[1], contract)
        + product(p[1], q[0], contract)
    )


def cost_half(left_parts, left_sq, right_ref, cost_ref, place):
    cols, width = right_ref.shape
    right = right_ref[...]
    right_parts = parts_of(right)
    cross = sum(product(left_parts[p][...], right_parts[q], (1, 1)) for p, q in PASSES)
    ones = jnp.ones((8, width), jnp.bfloat16)
    right_sq = sum(product(ones, part, (1, 1)) for part in parts_of(right * right))[:1]
    at = pl.ds(pl.multiple_of(place * cols, LANES), cols)
    cost_ref[:, at] = (left_sq + right_sq - 2.0 * cross) / width


def mine_kernel(*refs):
    pieces, mine_hbm = refs[:2], refs[2]
    src_out, high_ref, mid_ref, low_ref, sq_ref, cost_ref = refs[3:9]
    src_ref, mine_ref, sem, out_sem = refs[9:]
    x, c = (lax.axis_index(name) for name in ("x", "c"))
    a = x // 2
    half = pieces[0].shape[0]
    copies = [pltpu.make_async_copy(mine_hbm, mine_ref, sem.at[2])]
    for side, place in enumerate((a, 1 - a)):
        at = pl.multiple_of(place * half, 8)
        copies.append(
            pltpu.make_async_copy(pieces[side], src_ref.at[pl.ds(at, half)], sem.at[side])
        )
    for copy in copies:
        copy.start()
    for copy in copies:
        copy.wait()
    out = pltpu.make_async_copy(src_ref, src_out, out_sem)
    out.start()
    left = src_ref[...]
    left_sq = jnp.sum(left * left, axis=1, keepdims=True)
    sq_ref[...] = left_sq
    high_ref[...], mid_ref[...], low_ref[...] = parts_of(left)
    cost_half((high_ref, mid_ref, low_ref), left_sq, mine_ref, cost_ref, c)
    out.wait()


def other_kernel(high_ref, mid_ref, low_ref, sq_ref, other_ref, same_ref, cost_ref):
    del same_ref
    place = 1 - lax.axis_index("c")
    cost_half((high_ref, mid_ref, low_ref), sq_ref[...], other_ref, cost_ref, place)


def tile(row_pieces, mine):
    width = mine.shape[1]
    rows, cols = 2 * row_pieces[0].shape[0], 2 * mine.shape[0]
    part = jax.ShapeDtypeStruct((rows, width), jnp.bfloat16)
    src_block, high, mid, low, left_sq, cost = pl.pallas_call(
        mine_kernel,
        out_shape=(
            jax.ShapeDtypeStruct((rows, width), jnp.float32),
            part,
            part,
            part,
            jax.ShapeDtypeStruct((rows, 1), jnp.float32),
            jax.ShapeDtypeStruct((rows, cols), jnp.float32),
        ),
        in_specs=[IN_HBM] * 3,
        out_specs=(IN_HBM,) + (WHOLE,) * 5,
        scratch_shapes=[
            pltpu.VMEM((rows, width), jnp.float32),
            pltpu.VMEM(mine.shape, jnp.float32),
            pltpu.SemaphoreType.DMA((3,)),
            pltpu.SemaphoreType.DMA,
        ],
        compiler_params=pltpu.CompilerParams(vmem_limit_bytes=VMEM_LIMIT),
    )(*row_pieces, mine)
    other = lax.ppermute(mine, "c", SWAP)
    cost = pl.pallas_call(
        other_kernel,
        out_shape=jax.ShapeDtypeStruct((rows, cols), jnp.float32),
        in_specs=[WHOLE] * 6,
        out_specs=WHOLE,
        input_output_aliases={5: 0},
        compiler_params=pltpu.CompilerParams(vmem_limit_bytes=VMEM_LIMIT),
    )(high, mid, low, left_sq, other, cost)
    return src_block, other, cost


def half_of(high_ref, mid_ref, place):
    size = high_ref.shape[1] // 2
    at = pl.ds(pl.multiple_of(place * size, LANES), size)
    return high_ref[:, at], mid_ref[:, at]


def pull(weight_parts, src_ref, tgt):
    pulled = three_products(weight_parts, parts_of(src_ref[...]), (0, 0))
    ones = jnp.ones((src_ref.shape[0], LANES), jnp.bfloat16)
    mass = sum(product(part, ones, (0, 0)) for part in weight_parts)[:, :1]
    return mass * tgt - pulled


def send_kernel(
    src_pot_ref, tgt_pot_ref, cost_ref, src_hbm, other_hbm, sent_ref, high_ref, mid_ref,
    src_ref, tgt_ref, sem,
):
    rows, cols = cost_ref.shape
    copies = (
        pltpu.make_async_copy(src_hbm, src_ref, sem.at[0]),
        pltpu.make_async_copy(other_hbm, tgt_ref, sem.at[1]),
    )
    for copy in copies:
        copy.start()
    lane = lax.broadcasted_iota(jnp.int32, (LANES, LANES), 1)
    sub = lax.broadcasted_iota(jnp.int32, (LANES, LANES), 0)
    for i in range(rows // LANES):
        at = slice(i * LANES, (i + 1) * LANES)
        row = jnp.broadcast_to(src_pot_ref[:, at], (LANES, LANES))
        column = jnp.sum(jnp.where(lane == sub, row, 0.0), axis=1, keepdims=True)
        for j in range(cols // LANES):
            to = slice(j * LANES, (j + 1) * LANES)
            total = column + tgt_pot_ref[:, to] - cost_ref[at, to]
            weight = jnp.exp(total / ENTROPY_REG)
            high = weight.astype(jnp.bfloat16)
            high_ref[at, to] = high
            mid_ref[at, to] = (weight - high.astype(jnp.float32)).astype(jnp.bfloat16)
    for copy in copies:
        copy.wait()
    place = 1 - lax.axis_index("c")
    sent_ref[...] = pull(half_of(high_ref, mid_ref, place), src_ref, tgt_ref[...])


def push_kernel(high_ref, mid_ref, src_ref, mine_ref, other_ref, *out_refs):
    out_refs, part_ref = out_refs[:-1], out_refs[-1]
    y, c = lax.axis_index("y"), lax.axis_index("c")
    ones = jnp.ones((mine_ref.shape[0], LANES), jnp.bfloat16)
    pushed, mass = 0.0, 0.0
    for place, ref in ((c, mine_ref), (1 - c, other_ref)):
        weight_parts = half_of(high_ref, mid_ref, place)
        pushed += three_products(weight_parts, parts_of(ref[...]), (1, 0))
        mass += sum(product(part, ones, (1, 0)) for part in weight_parts)
    part_ref[...] = mass[:, :1] * src_ref[...] - pushed
    size = out_refs[0].shape[1]
    for k, ref in zip(STEPS + (0,), out_refs):
        for a in range(2):
            at = pl.multiple_of((a * NY + (y + k) % NY) * size, 8)
            ref[a] = part_ref[pl.ds(at, size), :]


def keep_kernel(high_ref, mid_ref, src_ref, mine_ref, came_ref, out_ref):
    place = lax.axis_index("c")
    kept = pull(half_of(high_ref, mid_ref, place), src_ref, mine_ref[...])
    out_ref[...] = kept + came_ref[...]


def on_tile(kernel, out_shape, scratch, *args):
    return pl.pallas_call(
        kernel,
        out_shape=out_shape,
        in_specs=[WHOLE] * len(args),
        out_specs=jax.tree.map(lambda _: WHOLE, out_shape),
        scratch_shapes=scratch,
        compiler_params=pltpu.CompilerParams(vmem_limit_bytes=VMEM_LIMIT),
    )(*args)


def exchange(local, axes, groups, count):
    flat = local.reshape(1, 1, local.size)
    got = all_to_all(jnp.broadcast_to(flat, (count, 1, local.size)), axes, groups)
    peak = jnp.max(got, axis=0)
    total = jnp.sum(jnp.exp(got - peak[None]), axis=0)
    return peak + jnp.log(total)


def local_lse(scores, axis):
    peak = jnp.max(scores, axis=axis, keepdims=True)
    total = jnp.sum(jnp.exp(scores - peak), axis=axis)
    return jnp.squeeze(peak, axis) + jnp.log(total)


def per_device(src_emb, tgt_emb):
    rows, width = src_emb.shape
    z, x, y, c = (lax.axis_index(name) for name in ("z", "x", "y", "c"))
    a = x // 2
    b = (x // 2) ^ (x % 2)
    total_points = rows * NZ * NX * NY * NC
    mine = gather_blocks(tgt_emb, ("z", "x"), SIDE_GROUPS)
    near = lax.all_gather(src_emb, "y", axis=0, tiled=True)
    far = lax.ppermute(near, "x", FLIP_A)
    mine, far = lax.optimization_barrier((mine, far))
    src_block, other, cost = tile((near, far), mine)
    tile_rows, tile_cols = cost.shape
    tgt_pot = jnp.zeros((tile_cols,), jnp.float32)
    log_total = math.log(total_points)
    for _ in range(ITERS):
        lse = local_lse((tgt_pot.reshape(1, tile_cols) - cost) / ENTROPY_REG, 1)
        lse = exchange(lse, ("x", "y"), ROW_GROUPS, 2 * NY)
        src_pot = -ENTROPY_REG * (lse - log_total)
        lse = local_lse((src_pot.reshape(tile_rows, 1) - cost) / ENTROPY_REG, 0)
        lse = exchange(lse, ("z", "x", "c"), COL_GROUPS, 2 * NZ * NC)
        tgt_pot = -ENTROPY_REG * (lse - log_total)
    part = jax.ShapeDtypeStruct(cost.shape, jnp.bfloat16)
    half = jax.ShapeDtypeStruct(mine.shape, jnp.float32)
    sent, high, mid = pl.pallas_call(
        send_kernel,
        out_shape=(half, part, part),
        in_specs=[WHOLE] * 3 + [IN_HBM] * 2,
        out_specs=(WHOLE,) * 3,
        scratch_shapes=[
            pltpu.VMEM(src_block.shape, jnp.float32),
            pltpu.VMEM(mine.shape, jnp.float32),
            pltpu.SemaphoreType.DMA((2,)),
        ],
        compiler_params=pltpu.CompilerParams(vmem_limit_bytes=VMEM_LIMIT),
    )(src_pot, tgt_pot, cost, src_block, other)
    came = lax.ppermute(sent, "c", SWAP)
    pair = jax.ShapeDtypeStruct((2, rows, width), jnp.float32)
    scratch = [pltpu.VMEM(src_block.shape, jnp.float32)]
    pieces = on_tile(push_kernel, (pair,) * NY, scratch, high, mid, src_block, mine, other)
    pieces = list(pieces)
    came, pieces[0] = lax.optimization_barrier((came, pieces[0]))
    tgt_half = on_tile(keep_kernel, half, [], high, mid, src_block, mine, came)
    tgt_sum = scatter_blocks(tgt_half, ("z", "x"), SIDE_GROUPS)
    src_sum = scatter_ring(pieces, a)
    src_piece = take(src_pot.reshape(-1, rows), a * NY + y)
    tgt_piece = take(tgt_pot.reshape(-1, rows), (c * 2 + b) * NZ + z)
    return src_piece, tgt_piece, src_sum / total_points, tgt_sum / total_points


def solution(mesh):
    grid = Mesh(mesh.devices.reshape(NZ, NX, NY, NC), ("z", "x", "y", "c"))
    split = ("z", "x", "y", "c")
    return jax.shard_map(
        per_device,
        mesh=grid,
        in_specs=(P(split, None), P(split, None)),
        out_specs=(P(split), P(split), P(split, None), P(split, None)),
        check_vma=False,
    )
```
